32 devices in a mesh: cluster: 8 (over z, x), tile: 4 (over y, core).
Axes of the slice: x: 2, y: 2, z: 4, core: 2. Of those that a mesh axis runs over, the one named last changes fastest.
Arguments:
- points: bfloat16 [64, 8, 512], P('cluster', None, 'tile'), as said below
- charges: bfloat16 [64, 512, 256], P('cluster', 'tile'), may hold values from -6 to 6
- near_ids: int32 [64, 8], P('cluster'), may hold values from 0 to 63, as said below
- near_count: int32 [64], P('cluster'), may hold values from 1 to 8, as said below
- leaf_pivots: int32 [64, 256], P('cluster'), may hold values from 0 to 511, as said below
- merge_pivots: int32 [32, 6, 256], P('cluster'), may hold values from 0 to 511, as said below
Outputs:
- near_field: bfloat16 [64, 512, 256], P('cluster', 'tile')
- top_weights: bfloat16 [8, 256, 256], P('cluster', None, 'tile')
The draws below stay inside these ranges and needn't reach their ends.
Inputs may be any that keep to these rules, and one draw needn't show every extreme that they name: `near_ids`: slot 0 of box b holds b itself and slots from near_count[b] on repeat b; the other used slots name distinct boxes other than b at most 4 boxes away from b; some box names a box exactly 4 away. `near_count`: some box uses all 8 slots. `leaf_pivots`: the pivots of a box are distinct. `merge_pivots`: the pivots of a row are distinct; rows q and q2 of level l are equal when q // 2^l == q2 // 2^l. The points of a box lie around a centre that moves along a smooth curve with the box number.
All inputs are finite; a program needn't handle non-finite values.
Results may differ from the reference program's by a relative error of at most 0.005.
Values may be sent and summed in bfloat16 or wider, within the bound.
No kernel may reach another device: no remote copies, remote signals or barrier semaphores. Data moves between devices by JAX's collectives and lax.ppermute only.
A program may use at most 192 MiB of HBM per device.

```python
import jax
import jax.numpy as jnp
from jax import lax

FEAT = 8
LEAF = 512
RANK = 256
R = 256
LEAF_DEV = 8
LEVELS = 6
MOST = 8
SPAN = 4
BOXES = 64
N_CLUSTER = 8


def draw_points(key, part):
    shape = (BOXES, FEAT, LEAF)
    key_phase, key_spread = jax.random.split(jax.random.fold_in(key, 3))
    phases = jax.random.uniform(key_phase, (FEAT,), jnp.float32, -3.1, 3.1)
    rates = 0.02 + 0.004 * jnp.arange(FEAT).astype(jnp.float32)
    box_numbers = jnp.arange(BOXES).astype(jnp.float32)
    centres = 4.0 * jnp.sin(box_numbers[:, None] * rates[None, :] + phases[None, :])
    spread = 0.3 * jax.random.truncated_normal(key_spread, -4.0, 4.0, shape, jnp.float32)
    values = centres[:, :, None] + spread
    return values.astype(jnp.bfloat16)


def near_lists(key):
    base_key = jax.random.fold_in(key, 71)
    key_scores, key_heavy, key_light = jax.random.split(base_key, 3)
    offsets = jnp.concatenate([jnp.arange(-SPAN, 0), jnp.arange(1, SPAN + 1)]).astype(jnp.int32)
    box_numbers = jnp.arange(BOXES).astype(jnp.int32)
    candidates = box_numbers[:, None] + offsets[None, :]
    in_range = (candidates >= 0) & (candidates < BOXES)
    positions = jnp.arange(2 * SPAN).astype(jnp.int32)[None, :]
    scores = jax.random.randint(key_scores, candidates.shape, 0, 1000) * 64 + positions
    scores = jnp.where(in_range, scores, -1 - positions)
    ranking = jnp.argsort(-scores, axis=1, stable=True)
    picked = jnp.take_along_axis(candidates, ranking, axis=1)[:, :MOST - 1]
    available = jnp.sum(in_range.astype(jnp.int32), axis=1) + 1
    heavy_device = jax.random.randint(key_heavy, (N_CLUSTER,), 0, 8) == 0
    heavy_device = heavy_device.at[N_CLUSTER // 2].set(True)
    heavy_box = jnp.repeat(heavy_device, LEAF_DEV)
    light_count = jax.random.randint(key_light, (BOXES,), 1, 4)
    near_counts = jnp.minimum(jnp.where(heavy_box, MOST, light_count), available).astype(jnp.int32)
    slot_numbers = jnp.arange(1, MOST)[None, :]
    rest = jnp.where(slot_numbers < near_counts[:, None], picked, box_numbers[:, None])
    identities = jnp.concatenate([box_numbers[:, None], rest], axis=1).astype(jnp.int32)
    return (identities, near_counts)


def draw_near_ids(key, part):
    return near_lists(key)[0]


def draw_near_count(key, part):
    return near_lists(key)[1]


def draw_leaf_pivots(key, part):
    box_keys = jax.random.split(jax.random.fold_in(key, 5), BOXES)
    shuffled = jax.vmap(lambda single: jax.random.permutation(single, LEAF))(box_keys)
    return shuffled[:, :RANK].astype(jnp.int32)


def draw_merge_pivots(key, part):
    pair_count = BOXES // 2
    box_keys = jax.random.split(jax.random.fold_in(key, 9), LEVELS * pair_count)
    shuffled = jax.vmap(lambda single: jax.random.permutation(single, 2 * RANK))(box_keys)
    shuffled = shuffled.reshape(LEVELS, pair_count, 2 * RANK)[:, :, :RANK]
    owner_rows = jnp.arange(pair_count)[:, None] // (2 ** jnp.arange(LEVELS))[None, :]
    level_numbers = jnp.arange(LEVELS)[None, :]
    return shuffled[level_numbers, owner_rows].astype(jnp.int32)


def levels(rng, dims, cuts, low, largest):
    loudness = 1.0
    for axis_at, blocks in cuts:
        heights = jax.random.uniform(jax.random.fold_in(jax.random.fold_in(rng, 6), axis_at), (blocks,), jnp.float32, low / len(cuts), largest / len(cuts))
        loudness = loudness * jnp.repeat(jnp.exp(heights), dims[axis_at] // blocks).reshape((-1,) + (1,) * (len(dims) - 1 - axis_at))
    return loudness


def normal_values(rng, extent, scale, bound, cuts=(), held_as=jnp.bfloat16):
    loudness = levels(rng, extent, cuts, -0.22, 0.18) if cuts else 1.0
    values = jax.random.normal(rng, extent, jnp.float32) * scale * loudness
    return jnp.minimum(jnp.maximum(values, -bound), bound).astype(held_as)


def setup_inputs(seed: int = 0) -> dict:
    seeds = jax.random.split(jax.random.key(seed), 7)
    points = draw_points(jax.random.fold_in(seeds[6], 71), 0)
    charges = normal_values(seeds[1], (BOXES, LEAF, R), 1.0, 6.0, ((0, 8), (1, 4)))
    near_ids = draw_near_ids(jax.random.fold_in(seeds[6], 71), 0)
    near_count = draw_near_count(jax.random.fold_in(seeds[6], 71), 0)
    leaf_pivots = draw_leaf_pivots(jax.random.fold_in(seeds[6], 71), 0)
    merge_pivots = draw_merge_pivots(jax.random.fold_in(seeds[6], 71), 0)
    return {"points": points, "charges": charges, "near_ids": near_ids, "near_count": near_count, "leaf_pivots": leaf_pivots, "merge_pivots": merge_pivots}


lengthscale = 0.7

def kernel_tile(left_set, right_set):
    left_wide = left_set.astype(jnp.float32)
    right_wide = right_set.astype(jnp.float32)
    squares = jnp.zeros((left_set.shape[1], right_set.shape[1]), jnp.float32)
    for feature in range(left_set.shape[0]):
        difference = left_wide[feature][:, None] - right_wide[feature][None, :]
        squares = squares + difference * difference
    return jnp.exp(-jnp.sqrt(squares) / lengthscale)

def merge_level(cand_coords, cand_weights, pivots):
    chosen = jnp.take(cand_coords, pivots, axis=1)
    tile_values = kernel_tile(chosen, cand_coords).astype(jnp.bfloat16)
    merged = jnp.dot(tile_values, cand_weights, preferred_element_type=jnp.float32).astype(jnp.bfloat16)
    return (chosen, merged)

def reference(points, charges, near_ids, near_count, leaf_pivots, merge_pivots):

    def near_one(box_index):
        own_coords = points[box_index]
        running = jnp.zeros((LEAF, R), jnp.float32)
        for slot_index in range(MOST):
            neighbour = near_ids[box_index, slot_index]
            live_slot = slot_index < near_count[box_index]
            neighbour_charges = jnp.where(live_slot, charges[neighbour], jnp.zeros((LEAF, R), charges.dtype))
            tile_values = kernel_tile(own_coords, points[neighbour]).astype(jnp.bfloat16)
            running = running + jnp.dot(tile_values, neighbour_charges, preferred_element_type=jnp.float32)
        return running.astype(jnp.bfloat16)
    near_field = lax.map(near_one, jnp.arange(BOXES).astype(jnp.int32))

    def apply_merge(operands):
        return merge_level(operands[0], operands[1], operands[2])
    coords, weights = lax.map(apply_merge, (points, charges, leaf_pivots))
    for level_index in range(LEVELS):
        stride = 2 ** level_index
        cand_coords = jnp.concatenate([coords[0::2], coords[1::2]], axis=2)
        cand_weights = jnp.concatenate([weights[0::2], weights[1::2]], axis=1)
        level_pivots = merge_pivots[0::stride, level_index]
        coords, weights = lax.map(apply_merge, (cand_coords, cand_weights, level_pivots))
    top_weights = jnp.repeat(weights, 2 ** LEVELS // LEAF_DEV, axis=0)
    return (near_field, top_weights)
```

```python
import functools
import math

import jax
import jax.numpy as jnp
from jax import lax
from jax.experimental import pallas as pl
from jax.experimental.pallas import tpu as pltpu
from jax.sharding import PartitionSpec as P

SPAN = 4
lengthscale = 0.7
KAPPA = math.log2(math.e) / lengthscale
FLOOR = 1e-30
VMEM_LIMIT = 48 * 1024 * 1024
f32 = jnp.float32
bf16 = jnp.bfloat16
VMEM = pl.BlockSpec(memory_space=pltpu.VMEM)
SMEM = pl.BlockSpec(memory_space=pltpu.SMEM)


def features(coords, centre):
    shifted = (coords - centre) * KAPPA
    high = shifted.astype(bf16).astype(f32)
    low = (shifted - high).astype(bf16).astype(f32)
    both = high + low
    norm = jnp.sum(both * both, axis=0, keepdims=True)
    first = norm.astype(bf16).astype(f32)
    second = (norm - first).astype(bf16).astype(f32)
    third = norm - first - second
    row = lax.broadcasted_iota(jnp.int32, coords.shape, 0)
    one = jnp.ones_like(coords)
    nil = jnp.zeros_like(coords)

    def six(a, b, c, d, e, f):
        out = jnp.where(row == 0, a, jnp.where(row == 1, b, jnp.where(row == 2, c, nil)))
        return jnp.where(row == 3, d, jnp.where(row == 4, e, jnp.where(row == 5, f, out)))

    left = [-2 * high, -2 * high, -2 * low, -2 * low, six(first, second, third, one, one, one), nil]
    right = [high, low, high, low, six(one, one, one, first, second, third), nil]
    return jnp.concatenate(left, axis=0), jnp.concatenate(right, axis=0).astype(bf16)


def kernel_values(squares):
    squares = jnp.maximum(squares, FLOOR)
    return jnp.exp2(-(squares * lax.rsqrt(squares))).astype(bf16)


def dot(a, b):
    return jnp.dot(a, b, preferred_element_type=f32)


def choose(coords, pivots):
    place = lax.broadcasted_iota(jnp.int32, (coords.shape[1], pivots.shape[1]), 0)
    return dot(coords.astype(bf16), jnp.where(place == pivots, 1.0, 0.0).astype(bf16))


def lanes(*parts):
    return jnp.concatenate(parts, axis=1)


def centre_of(coords):
    return jnp.mean(coords.astype(f32), axis=1, keepdims=True)


def tree_kernel(info, pts0, pts1, pts2, pts3, own, mate, leaf_pv, merge_pv, out, held):
    half = leaf_pv.shape[0]
    group = info[1]
    tile = info[2]
    first = group * half
    points = [pts0, pts1, pts2, pts3]
    centre = centre_of(pts0[first + half // 2])
    coords, weights = [], []
    for i in range(half):
        box = first + i
        own_pts = pts0[box].astype(f32)
        mate_pts = pts1[box].astype(f32)
        whole = lanes(own_pts, mate_pts, pts2[box].astype(f32), pts3[box].astype(f32))
        chosen = choose(whole, leaf_pv[i : i + 1, :] ^ (tile * own_pts.shape[1]))
        left, _ = features(chosen, centre)
        _, right = features(lanes(own_pts, mate_pts), centre)
        values = kernel_values(dot(left.T.astype(bf16), right))
        charge = jnp.concatenate([own[box], mate[box]], axis=0)
        coords.append(chosen)
        weights.append(dot(values, charge).astype(bf16))
    level = 0
    row = 0
    while len(coords) > 1:
        next_coords, next_weights = [], []
        for i in range(len(coords) // 2):
            cand = lanes(coords[2 * i], coords[2 * i + 1])
            chosen = choose(cand, merge_pv[row : row + 1, :])
            row += 1
            left, _ = features(chosen, centre)
            _, right = features(cand, centre)
            values = kernel_values(dot(left.T.astype(bf16), right))
            charge = jnp.concatenate([weights[2 * i], weights[2 * i + 1]], axis=0)
            next_coords.append(chosen)
            next_weights.append(dot(values, charge))
        coords = next_coords
        if len(coords) > 1:
            weights = [w.astype(bf16) for w in next_weights]
        else:
            weights = next_weights
        level += 1
    held[...] = weights[0].T
    width = out.shape[1] - 16
    extra = jnp.concatenate([coords[0], jnp.zeros_like(coords[0])], axis=0).astype(bf16)
    for d in range(4):
        part = held[pl.ds(pl.multiple_of((tile ^ d) * width, width), width), :]
        out[d] = jnp.concatenate([part.astype(bf16), extra], axis=0)


def merge_body(cand_coords, cand_weights, pivots):
    chosen = choose(cand_coords, pivots)
    across = cand_coords.T
    squares = None
    for f in range(cand_coords.shape[0]):
        diff = across[:, f : f + 1] - chosen[f : f + 1, :]
        squares = diff * diff if squares is None else squares + diff * diff
    values = kernel_values(squares * (KAPPA * KAPPA))
    return chosen, dot(cand_weights, values)


def join_kernel(info, mine, got1, got2, got3, pivots, out):
    width = out.shape[0] - 16
    ours = (mine[:width, :].astype(f32) + got2[:width, :].astype(f32)).astype(bf16)
    theirs = (got1[:width, :].astype(f32) + got3[:width, :].astype(f32)).astype(bf16)
    coords = lanes(mine[width:, :].astype(f32)[:8], got1[width:, :].astype(f32)[:8])
    chosen, merged = merge_body(coords, lanes(ours, theirs), pivots[...] ^ (info[1] * mine.shape[1]))
    extra = jnp.concatenate([chosen, jnp.zeros_like(chosen)], axis=0)
    out[...] = jnp.concatenate([merged, extra], axis=0).astype(bf16)


def level_kernel(last, info, mine, got, pivots, out):
    width = mine.shape[0] - 16
    coords = lanes(mine[width:, :].astype(f32)[:8], got[width:, :].astype(f32)[:8])
    weights = lanes(mine[:width, :], got[:width, :])
    chosen, merged = merge_body(coords, weights, pivots[...] ^ (info[0] * mine.shape[1]))
    if last:
        out[...] = merged.T.astype(bf16)
    else:
        extra = jnp.concatenate([chosen, jnp.zeros_like(chosen)], axis=0)
        out[...] = jnp.concatenate([merged, extra], axis=0).astype(bf16)


def near_own_kernel(info, ids, count, pts0, pts1, pts2, pts3, own, mate, out, right_ref, left_ref):
    boxes = own.shape[0]
    half = out.shape[0]
    group = info[1]
    base = info[0]
    centre = centre_of(pts0[group * half + half // 2])
    for n in range(boxes):
        right_ref[n] = features(lanes(pts0[n], pts1[n]).astype(f32), centre)[1]

    def one(n):
        charge = jnp.concatenate([own[n], mate[n]], axis=0)
        return dot(kernel_values(dot(left_ref[...], right_ref[n])), charge)

    def box_step(u, _):
        box = group * half + u
        whole = lanes(pts0[box], pts1[box], pts2[box], pts3[box]).astype(f32)
        left_ref[...] = features(whole, centre)[0].T.astype(bf16)
        out[u] = one(box)

        def slot_step(slot, _):
            n = ids[box, slot] - base

            @pl.when((n >= 0) & (n < boxes))
            def _():
                out[u] += one(n)

            return 0

        lax.fori_loop(1, count[box], slot_step, 0)
        return 0

    lax.fori_loop(0, half, box_step, 0)


def near_halo_kernel(part, info, ids, count, pts0, pts1, pts2, pts3, total, *rest):
    halos = rest[: 2 * (part + 1)]
    keep, send, right_ref, left_ref, acc = rest[2 * (part + 1) :]
    boxes = pts0.shape[0]
    half = boxes // 2
    pair = half // 2
    group = info[1]
    base = info[0]
    centre = centre_of(pts0[group * half + half // 2])
    for k in range(part + 1):
        for i in range(pair):
            right_ref[k * pair + i] = features(halos[2 * k][i].astype(f32), centre)[1]
    start = jnp.where(group == 0, (1 - part) * pair, part * pair)
    rows = pts0.shape[2]

    def box_step(v, _):
        u = start + v
        box = group * half + u
        whole = lanes(pts0[box], pts1[box], pts2[box], pts3[box]).astype(f32)
        left_ref[...] = features(whole, centre)[0].T.astype(bf16)
        acc[...] = total[u]

        def slot_step(slot, _):
            n = ids[box, slot] - base

            @pl.when((n < 0) | (n >= boxes))
            def _():
                away = jnp.where(group == 0, -1 - n, n - boxes)
                chunk = away // pair
                inside = jnp.where(group == 0, pair - 1 - away % pair, away % pair)
                for k in range(part + 1):

                    @pl.when(chunk == k)
                    def _():
                        values = kernel_values(dot(left_ref[...], right_ref[k * pair + inside]))
                        acc[...] += dot(values, halos[2 * k + 1][inside])

            return 0

        lax.fori_loop(1, count[box], slot_step, 0)
        keep[v] = acc[:rows, :]
        for d in range(1, 4):
            send[d - 1, v] = acc[d * rows : (d + 1) * rows, :].astype(bf16)
        return 0

    lax.fori_loop(0, pair, box_step, 0)


def call(body, out_shape, n_smem, n_vmem, scratch=()):
    return pl.pallas_call(
        body,
        out_shape=out_shape,
        in_specs=[SMEM] * n_smem + [VMEM] * n_vmem,
        out_specs=jax.tree.map(lambda _: VMEM, out_shape),
        scratch_shapes=list(scratch),
        compiler_params=pltpu.CompilerParams(vmem_limit_bytes=VMEM_LIMIT),
    )


def on_device(points, charges, near_ids, near_count, leaf_pivots, merge_pivots):
    boxes, feat, rows = points.shape
    probes = charges.shape[2]
    rank = leaf_pivots.shape[1]
    half = boxes // 2
    pair = half // 2
    tiles = lax.axis_size("tile")
    clusters = lax.axis_size("cluster")
    c = lax.axis_index("cluster")
    t = lax.axis_index("tile")
    group = t % 2
    base = c * boxes
    info = jnp.stack([base, group, t]).astype(jnp.int32)

    def to_tile(x, d):
        return lax.ppermute(x, "tile", [(i, i ^ d) for i in range(tiles)])

    def to_halo(x):
        route = []
        for i in range(clusters):
            for k in range(tiles):
                target = i + 1 if k % 2 == 0 else i - 1
                if 0 <= target < clusters:
                    route.append((i * tiles + k, target * tiles + k))
        return lax.ppermute(x, ("cluster", "tile"), route)

    def partner(x, stride):
        route = [(i, i ^ stride) for i in range(clusters) if i ^ stride < clusters]
        return lax.ppermute(x, "cluster", route)

    pts = [points] + [to_tile(points, d) for d in range(1, 4)]
    mate = to_tile(charges, 1)

    halos = []
    for part in range(2):
        start = jnp.where(group == 0, boxes - (part + 1) * pair, part * pair)
        cut = lambda x: lax.dynamic_slice_in_dim(x, start, pair, 0)
        halo_pts = jnp.concatenate([cut(points), cut(pts[1])], axis=2)
        halo_charges = jnp.concatenate([cut(charges), cut(mate)], axis=1)
        halos += [to_halo(halo_pts), to_halo(halo_charges)]

    local_levels = boxes.bit_length() - 1
    leaf_pv = lax.dynamic_slice_in_dim(leaf_pivots, group * half, half, 0)
    pieces = []
    for level in range(local_levels - 1):
        stride = 2**level
        at_level = merge_pivots[::stride, level]
        pieces.append(lax.dynamic_slice_in_dim(at_level, group * (at_level.shape[0] // 2), at_level.shape[0] // 2, 0))
    merge_pv = jnp.concatenate(pieces, axis=0)
    width = probes // tiles
    tree = call(
        tree_kernel,
        jax.ShapeDtypeStruct((4, width + 16, rank), bf16),
        1,
        8,
        [pltpu.VMEM((probes, rank), f32)],
    )(info, *pts, charges, mate, leaf_pv, merge_pv)

    got = [to_tile(tree[d], d) for d in range(1, 4)]
    wide = call(join_kernel, jax.ShapeDtypeStruct((width + 16, rank), bf16), 1, 5)(
        info, tree[0], *got, merge_pivots[0, local_levels - 1][None]
    )

    out_shape = jax.ShapeDtypeStruct((half, 4 * rows, probes), f32)
    total = call(
        near_own_kernel,
        out_shape,
        3,
        6,
        [pltpu.VMEM((boxes, 48, 2 * rows), bf16), pltpu.VMEM((4 * rows, 48), bf16)],
    )(info, near_ids, near_count, *pts, charges, mate)

    levels_above = merge_pivots.shape[1] - local_levels
    for bit in range(levels_above):
        last = bit == levels_above - 1
        other = partner(wide, 2**bit)
        place = (c // 2**bit % 2).astype(jnp.int32)[None]
        shape = (rank, width) if last else (width + 16, rank)
        wide = call(functools.partial(level_kernel, last), jax.ShapeDtypeStruct(shape, bf16), 1, 3)(
            place, wide, other, merge_pivots[0, local_levels + bit][None]
        )

    sums = []
    for part in range(2):
        keep, send = call(
            functools.partial(near_halo_kernel, part),
            (
                jax.ShapeDtypeStruct((pair, rows, probes), f32),
                jax.ShapeDtypeStruct((3, pair, rows, probes), bf16),
            ),
            3,
            5 + 2 * (part + 1),
            [
                pltpu.VMEM((half, 48, 2 * rows), bf16),
                pltpu.VMEM((4 * rows, 48), bf16),
                pltpu.VMEM((4 * rows, probes), f32),
            ],
        )(info, near_ids, near_count, *pts, total, *halos[: 2 * (part + 1)])
        back = [to_tile(send[d - 1], d).astype(f32) for d in range(1, 4)]
        mine = (keep + back[1]).astype(bf16)
        theirs = (back[0] + back[2]).astype(bf16)
        low = jnp.where(group == 0, mine, theirs)
        high = jnp.where(group == 0, theirs, mine)
        sums.append((low, high))
    near_field = jnp.concatenate([sums[1][0], sums[0][0], sums[0][1], sums[1][1]], axis=0)
    return near_field, wide[None]


def solution(mesh):
    return jax.shard_map(
        on_device,
        mesh=mesh,
        in_specs=(
            P("cluster", None, "tile"),
            P("cluster", "tile", None),
            P("cluster", None),
            P("cluster"),
            P("cluster", None),
            P("cluster", None, None),
        ),
        out_specs=(P("cluster", "tile", None), P("cluster", None, "tile")),
        check_vma=False,
    )
```

```python
import functools
import math

import jax
import jax.numpy as jnp
from jax import lax
from jax.experimental import pallas as pl
from jax.experimental.pallas import tpu as pltpu
from jax.sharding import PartitionSpec as P

SPAN = 4
lengthscale = 0.7
KAPPA = math.log2(math.e) / lengthscale
FLOOR = 1e-30
VMEM_LIMIT = 16 * 1024 * 1024
f32 = jnp.float32
bf16 = jnp.bfloat16
VMEM = pl.BlockSpec(memory_space=pltpu.VMEM)
SMEM = pl.BlockSpec(memory_space=pltpu.SMEM)
ANY = pl.BlockSpec(memory_space=pl.ANY)


def features(coords, centre):
    shifted = (coords - centre) * KAPPA
    high = shifted.astype(bf16).astype(f32)
    low = (shifted - high).astype(bf16).astype(f32)
    both = high + low
    norm = jnp.sum(both * both, axis=0, keepdims=True)
    first = norm.astype(bf16).astype(f32)
    second = (norm - first).astype(bf16).astype(f32)
    third = norm - first - second
    row = lax.broadcasted_iota(jnp.int32, coords.shape, 0)
    one = jnp.ones_like(coords)
    nil = jnp.zeros_like(coords)

    def six(a, b, c, d, e, f):
        out = jnp.where(row == 0, a, jnp.where(row == 1, b, jnp.where(row == 2, c, nil)))
        return jnp.where(row == 3, d, jnp.where(row == 4, e, jnp.where(row == 5, f, out)))

    left = [-2 * high, -2 * high, -2 * low, -2 * low, six(first, second, third, one, one, one), nil]
    right = [high, low, high, low, six(one, one, one, first, second, third), nil]
    return jnp.concatenate(left, axis=0), jnp.concatenate(right, axis=0).astype(bf16)


def kernel_values(squares):
    squares = jnp.maximum(squares, FLOOR)
    return jnp.exp2(-(squares * lax.rsqrt(squares))).astype(bf16)


def dot(a, b):
    return jnp.dot(a, b, preferred_element_type=f32)


def choose(coords, pivots):
    place = lax.broadcasted_iota(jnp.int32, (coords.shape[1], pivots.shape[1]), 0)
    return dot(coords.astype(bf16), jnp.where(place == pivots, 1.0, 0.0).astype(bf16))


def lanes(*parts):
    return jnp.concatenate(parts, axis=1)


def centre_of(coords):
    return jnp.mean(coords.astype(f32), axis=1, keepdims=True)


def position():
    tile = lax.axis_index("tile")
    return lax.axis_index("cluster"), lax.rem(tile, 2), tile


def load_kernel(points, charges, points_out, charges_out):
    points_out[...] = points[...]
    charges_out[...] = charges[...]


def stage_kernel(points, got1, charges, mate, after2, after3, to_send, joined):
    boxes, feat, rows = got1.shape
    joined[:, :rows, :] = charges[...]
    joined[:, rows:, :] = mate[...]
    count = to_send.shape[0]
    start = jnp.where(position()[1] == 0, boxes - count, 0)
    for i in range(count):
        box = start + i
        to_send[i, :rows, :] = charges[box]
        to_send[i, rows : 2 * rows, :] = mate[box]
        coords = lanes(points[box], got1[box]).astype(f32)
        to_send[i, 2 * rows :, :] = jnp.concatenate([coords, jnp.zeros_like(coords)], axis=0).astype(bf16)


def with_coords(weights, coords):
    return jnp.concatenate([weights, coords, jnp.zeros_like(coords)], axis=0).astype(bf16)


def tree_kernel(pts0, pts1, pts2, pts3, joined, leaf_pv, merge_pv, *refs):
    outs, held = refs[:4], refs[4]
    half = leaf_pv.shape[0] // 2
    rows = pts0.shape[2]
    _, group, tile = position()
    centre = centre_of(pts0[half])
    coords, weights = [], []
    for i in range(half):
        box = group * half + i
        whole = lanes(pts0[box], pts1[box], pts2[box], pts3[box]).astype(f32)
        chosen = choose(whole, leaf_pv[pl.ds(box, 1), :] ^ (tile * rows))
        left, _ = features(chosen, centre)
        _, right = features(whole[:, : 2 * rows], centre)
        values = kernel_values(dot(left.T.astype(bf16), right))
        coords.append(chosen)
        weights.append(dot(values, joined[box]))
    level = 0
    while len(coords) > 1:
        next_coords, next_weights = [], []
        for i in range(len(coords) // 2):
            cand = lanes(coords[2 * i], coords[2 * i + 1])
            pair = group * (half // 2) + i * 2**level
            chosen = choose(cand, merge_pv[level, pl.ds(pair, 1), :])
            left, _ = features(chosen, centre)
            _, right = features(cand, centre)
            values = kernel_values(dot(left.T.astype(bf16), right))
            charge = jnp.concatenate([weights[2 * i], weights[2 * i + 1]], axis=0).astype(bf16)
            next_coords.append(chosen)
            next_weights.append(dot(values, charge))
        coords, weights = next_coords, next_weights
        level += 1
    held[...] = weights[0].T
    width = held.shape[0] // 4
    for d, out in enumerate(outs):
        out[...] = with_coords(held[pl.ds(pl.multiple_of((tile ^ d) * width, width), width), :], coords[0])


def merged_pair(ours, theirs, our_coords, their_coords, pivots):
    coords = lanes(our_coords.astype(f32)[:8], their_coords.astype(f32)[:8])
    chosen = choose(coords, pivots)
    across = coords.T
    squares = None
    for f in range(coords.shape[0]):
        diff = across[:, f : f + 1] - chosen[f : f + 1, :]
        squares = diff * diff if squares is None else squares + diff * diff
    values = kernel_values(squares * (KAPPA * KAPPA))
    return dot(lanes(ours, theirs), values), chosen


def join_kernel(level, mine, got1, got2, got3, merge_pv, after, out):
    width = mine.shape[0] - 16
    _, group, _ = position()
    ours = (mine[:width, :].astype(f32) + got2[:width, :].astype(f32)).astype(bf16)
    theirs = (got1[:width, :].astype(f32) + got3[:width, :].astype(f32)).astype(bf16)
    pivots = merge_pv[level, :1, :] ^ (group * mine.shape[1])
    out[...] = with_coords(*merged_pair(ours, theirs, mine[width:, :], got1[width:, :], pivots))


def merge_kernel(level, bit, last, mine, got, merge_pv, after, out):
    width = mine.shape[0] - 16
    upper = lax.rem(lax.div(lax.axis_index("cluster"), 2**bit), 2)
    pivots = merge_pv[level, :1, :] ^ (upper * mine.shape[1])
    merged, chosen = merged_pair(mine[:width, :], got[:width, :], mine[width:, :], got[width:, :], pivots)
    if last:
        out[0] = merged.astype(bf16)
    else:
        out[...] = with_coords(merged, chosen)


def collect(ids, count, base, boxes_of, wanted, place, pad, list_v, list_n):
    found = 0
    for v, box in enumerate(boxes_of):
        used = count[box]
        for slot in range(1, ids.shape[1]):
            n = ids[box, slot] - base
            list_v[found] = v
            list_n[found] = place(n)
            found = found + ((slot < used) & wanted(n)).astype(jnp.int32)
    for i in range(3):
        list_v[found + i] = 0
        list_n[found + i] = pad
    return lax.div(found + 3, 4)


def far_row(right):
    row = lax.broadcasted_iota(jnp.int32, right.shape, 0)
    return jnp.where(row == 35, 1e30, 0.0).astype(bf16)


def near_own_kernel(part, ids, count, pts0, pts1, pts2, pts3, joined, *refs):
    if part == 0:
        after, out, left_ref, right_ref, list_v, list_n = refs
    else:
        right_ref, after, out, left_ref, list_v, list_n = refs
    boxes = joined.shape[0]
    half = boxes // 2
    pair = half // 2
    cluster, group, _ = position()
    centre = centre_of(pts0[half])
    if part == 0:
        for n in range(boxes):
            right_ref[n] = features(lanes(pts0[n], pts1[n]).astype(f32), centre)[1]
        right_ref[boxes] = far_row(right_ref[0])
    order = [group * half + part * pair + v for v in range(pair)]
    for v, box in enumerate(order):
        whole = lanes(pts0[box], pts1[box], pts2[box], pts3[box]).astype(f32)
        left_ref[v] = features(whole, centre)[0].T.astype(bf16)

    def one(v, n):
        return dot(kernel_values(dot(left_ref[v], right_ref[n])), joined[jnp.minimum(n, boxes - 1)])

    for v, box in enumerate(order):
        out[v] = one(v, box)
    groups = collect(
        ids, count, cluster * boxes, order, lambda n: (n >= 0) & (n < boxes), lambda n: n, boxes, list_v, list_n
    )

    def step(i, _):
        for k in range(4):
            v = list_v[4 * i + k]
            out[v] += one(v, list_n[4 * i + k])
        return 0

    lax.fori_loop(0, groups, step, 0)


def near_halo_kernel(
    ids, count, pts0, total0, total1, left0, left1, halo, after, keep, send1, send2, send3, right_ref, left_ref, acc, list_v, list_n
):
    boxes, feat, rows = pts0.shape
    half = boxes // 2
    pair = half // 2
    cluster, group, _ = position()
    centre = centre_of(pts0[half])
    for h in range(half):
        right_ref[h] = features(halo[h, 2 * rows :, :].astype(f32)[:feat], centre)[1]
    right_ref[half] = far_row(right_ref[0])
    order = [group * half + v for v in range(half)]
    for part, (total, left) in enumerate(((total0, left0), (total1, left1))):
        acc[part * pair : (part + 1) * pair] = total[...]
        left_ref[part * pair : (part + 1) * pair] = left[...]
    groups = collect(
        ids,
        count,
        cluster * boxes,
        order,
        lambda n: (n < 0) | (n >= boxes),
        lambda n: jnp.where(group == 0, n + half, n - boxes),
        half,
        list_v,
        list_n,
    )

    def step(i, _):
        for k in range(4):
            v = list_v[4 * i + k]
            h = list_n[4 * i + k]
            values = kernel_values(dot(left_ref[v], right_ref[h]))
            acc[v] += dot(values, halo[jnp.minimum(h, half - 1), : 2 * rows, :])
        return 0

    lax.fori_loop(0, groups, step, 0)
    keep[...] = acc[:, :rows, :]
    for d, send in enumerate((send1, send2, send3)):
        send[...] = acc[:, (d + 1) * rows : (d + 2) * rows, :].astype(bf16)


def finish_kernel(keep, back1, back2, back3, near):
    half = near.shape[0] // 2
    _, group, _ = position()
    near[pl.ds(group * half, half)] = (keep[...] + back2[...].astype(f32)).astype(bf16)
    near[pl.ds((1 - group) * half, half)] = (back1[...].astype(f32) + back3[...].astype(f32)).astype(bf16)


def call(body, out_shape, specs, micros, scratch=()):
    return pl.pallas_call(
        body,
        out_shape=out_shape,
        in_specs=specs,
        out_specs=jax.tree.map(lambda _: VMEM, out_shape),
        scratch_shapes=list(scratch),
        compiler_params=pltpu.CompilerParams(vmem_limit_bytes=VMEM_LIMIT),
        cost_estimate=pl.CostEstimate(flops=int(micros * 1e6), bytes_accessed=1024, transcendentals=0),
    )


def on_device(points, charges, near_ids, near_count, leaf_pivots, merge_pivots):
    boxes, feat, rows = points.shape
    probes = charges.shape[2]
    rank = leaf_pivots.shape[1]
    half = boxes // 2
    pair = half // 2
    tiles = lax.axis_size("tile")
    clusters = lax.axis_size("cluster")
    local_levels = boxes.bit_length() - 1
    levels_above = merge_pivots.shape[1] - local_levels

    def to_tile(x, d):
        return lax.ppermute(x, "tile", [(i, i ^ d) for i in range(tiles)])

    def to_halo(x):
        route = []
        for i in range(clusters):
            for k in range(tiles):
                target = i + 1 if k % 2 == 0 else i - 1
                if 0 <= target < clusters:
                    route.append((i * tiles + k, target * tiles + k))
        return lax.ppermute(x, ("cluster", "tile"), route)

    def partner(x, stride):
        route = [(i, i ^ stride) for i in range(clusters) if i ^ stride < clusters]
        return lax.ppermute(x, "cluster", route)

    def shape(*dims, dtype=bf16):
        return jax.ShapeDtypeStruct(dims, dtype)

    got = [to_tile(points, d) for d in range(1, 4)]
    mate = to_tile(charges, 1)
    points, charges = call(
        load_kernel, (shape(*points.shape), shape(*charges.shape)), [VMEM, VMEM], 1
    )(points, charges)
    to_send, joined = call(
        stage_kernel, (shape(half, 2 * rows + 16, probes), shape(boxes, 2 * rows, probes)), [VMEM] * 4 + [ANY] * 2, 0.5
    )(points, got[0], charges, mate, got[1], got[2])
    halo = to_halo(to_send)
    pts = [points] + got

    merge_pv = jnp.transpose(merge_pivots, (1, 0, 2))
    width = probes // tiles
    wide_shape = shape(width + 16, rank)
    mine, *sends = call(tree_kernel, (wide_shape,) * 4, [VMEM] * 7, 3, [pltpu.VMEM((probes, rank), f32)])(
        *pts, joined, leaf_pivots, merge_pv
    )
    others = [to_tile(sends[d - 1], d) for d in range(1, 4)]

    lists = [pltpu.SMEM((half * near_ids.shape[1] + 4,), jnp.int32)] * 2

    def near_own(part, extra, after):
        out = (shape(pair, 4 * rows, probes, dtype=f32), shape(pair, 4 * rows, 48))
        if part == 0:
            out += (shape(boxes + 1, 48, 2 * rows),)
        specs = [SMEM] * 2 + [VMEM] * (5 + len(extra)) + [ANY]
        return call(functools.partial(near_own_kernel, part), out, specs, 4, lists)(
            near_ids, near_count, *pts, joined, *extra, after
        )

    total0, left0, right = near_own(0, [], mine)
    wide = call(functools.partial(join_kernel, local_levels - 1), wide_shape, [VMEM] * 5 + [ANY], 1.5)(
        mine, *others, merge_pv, left0
    )
    total1, left1 = near_own(1, [right], wide)
    def level_up(bit, wide, after):
        last = bit == levels_above - 1
        out = shape(1, width, rank) if last else wide_shape
        body = functools.partial(merge_kernel, local_levels + bit, bit, last)
        return call(body, out, [VMEM] * 3 + [ANY], 1.5)(wide, partner(wide, 2**bit), merge_pv, after)

    wide = level_up(0, wide, total1)
    keep, *sends = call(
        near_halo_kernel,
        (shape(half, rows, probes, dtype=f32),) + (shape(half, rows, probes),) * 3,
        [SMEM] * 2 + [VMEM] * 6 + [ANY],
        3,
        [
            pltpu.VMEM((half + 1, 48, 2 * rows), bf16),
            pltpu.VMEM((half, 4 * rows, 48), bf16),
            pltpu.VMEM((half, 4 * rows, probes), f32),
        ]
        + lists,
    )(near_ids, near_count, points, total0, total1, left0, left1, halo, wide)
    back = [to_tile(sends[d - 1], d) for d in range(1, 4)]

    for bit in range(1, levels_above):
        wide = level_up(bit, wide, keep)
    near = call(finish_kernel, shape(boxes, rows, probes), [VMEM] * 4, 1.5)(keep, *back)
    return near, jnp.swapaxes(wide, 1, 2)


def solution(mesh):
    return jax.shard_map(
        on_device,
        mesh=mesh,
        in_specs=(
            P("cluster", None, "tile"),
            P("cluster", "tile", None),
            P("cluster", None),
            P("cluster"),
            P("cluster", None),
            P("cluster", None, None),
        ),
        out_specs=(P("cluster", "tile", None), P("cluster", None, "tile")),
        check_vma=False,
    )
```

```python
import functools
import math

import jax
import jax.numpy as jnp
from jax import lax
from jax.experimental import pallas as pl
from jax.experimental.pallas import tpu as pltpu
from jax.sharding import PartitionSpec as P

SPAN = 4
lengthscale = 0.7
KAPPA = math.log2(math.e) / lengthscale
FLOOR = 1e-30
COST = dict(load=0.001, stage=0.001, tree=3, own=1, join=1, merge=1, halo=5, finish=0.001)
VMEM_LIMIT = 16 * 1024 * 1024
f32 = jnp.float32
bf16 = jnp.bfloat16
VMEM = pl.BlockSpec(memory_space=pltpu.VMEM)
SMEM = pl.BlockSpec(memory_space=pltpu.SMEM)
ANY = pl.BlockSpec(memory_space=pl.ANY)


def features(coords, centre):
    shifted = (coords - centre) * KAPPA
    high = shifted.astype(bf16).astype(f32)
    low = (shifted - high).astype(bf16).astype(f32)
    both = high + low
    norm = jnp.sum(both * both, axis=0, keepdims=True)
    first = norm.astype(bf16).astype(f32)
    second = (norm - first).astype(bf16).astype(f32)
    third = norm - first - second
    row = lax.broadcasted_iota(jnp.int32, coords.shape, 0)
    one = jnp.ones_like(coords)
    nil = jnp.zeros_like(coords)

    def six(a, b, c, d, e, f):
        out = jnp.where(row == 0, a, jnp.where(row == 1, b, jnp.where(row == 2, c, nil)))
        return jnp.where(row == 3, d, jnp.where(row == 4, e, jnp.where(row == 5, f, out)))

    left = [-2 * high, -2 * high, -2 * low, -2 * low, six(first, second, third, one, one, one), nil]
    right = [high, low, high, low, six(one, one, one, first, second, third), nil]
    return jnp.concatenate(left, axis=0), jnp.concatenate(right, axis=0).astype(bf16)


def kernel_values(squares):
    squares = jnp.maximum(squares, FLOOR)
    return jnp.exp2(-(squares * lax.rsqrt(squares))).astype(bf16)


def dot(a, b):
    return jnp.dot(a, b, preferred_element_type=f32)


def choose(coords, pivots):
    place = lax.broadcasted_iota(jnp.int32, (coords.shape[1], pivots.shape[1]), 0)
    return dot(coords.astype(bf16), jnp.where(place == pivots, 1.0, 0.0).astype(bf16))


def lanes(*parts):
    return jnp.concatenate(parts, axis=1)


def centre_of(coords):
    return jnp.mean(coords.astype(f32), axis=1, keepdims=True)


def position():
    tile = lax.axis_index("tile")
    return lax.axis_index("cluster"), lax.rem(tile, 2), tile


def load_kernel(charges, out):
    out[...] = charges[...]


def stage_kernel(points, got1, charges, mate, after, to_send, joined):
    boxes, feat, rows = got1.shape
    joined[:, :rows, :] = charges[...]
    joined[:, rows:, :] = mate[...]
    count = to_send.shape[0]
    start = jnp.where(position()[1] == 0, boxes - count, 0)
    for i in range(count):
        box = start + i
        to_send[i, :rows, :] = charges[box]
        to_send[i, rows : 2 * rows, :] = mate[box]
        coords = lanes(points[box], got1[box]).astype(f32)
        to_send[i, 2 * rows :, :] = jnp.concatenate([coords, jnp.zeros_like(coords)], axis=0).astype(bf16)


def with_coords(weights, coords):
    return jnp.concatenate([weights, coords, jnp.zeros_like(coords)], axis=0).astype(bf16)


def tree_kernel(pts0, pts1, pts2, pts3, joined, leaf_pv, merge_pv, *refs):
    outs, held = refs[:4], refs[4]
    half = leaf_pv.shape[0] // 2
    rows = pts0.shape[2]
    _, group, tile = position()
    centre = centre_of(pts0[half])
    coords, weights = [], []
    for i in range(half):
        box = group * half + i
        whole = lanes(pts0[box], pts1[box], pts2[box], pts3[box]).astype(f32)
        chosen = choose(whole, leaf_pv[pl.ds(box, 1), :] ^ (tile * rows))
        left, _ = features(chosen, centre)
        _, right = features(whole[:, : 2 * rows], centre)
        values = kernel_values(dot(left.T.astype(bf16), right))
        coords.append(chosen)
        weights.append(dot(values, joined[box]))
    level = 0
    while len(coords) > 1:
        next_coords, next_weights = [], []
        for i in range(len(coords) // 2):
            cand = lanes(coords[2 * i], coords[2 * i + 1])
            pair = group * (half // 2) + i * 2**level
            chosen = choose(cand, merge_pv[level, pl.ds(pair, 1), :])
            left, _ = features(chosen, centre)
            _, right = features(cand, centre)
            values = kernel_values(dot(left.T.astype(bf16), right))
            charge = jnp.concatenate([weights[2 * i], weights[2 * i + 1]], axis=0).astype(bf16)
            next_coords.append(chosen)
            next_weights.append(dot(values, charge))
        coords, weights = next_coords, next_weights
        level += 1
    held[...] = weights[0].T
    width = held.shape[0] // 4
    for d, out in enumerate(outs):
        out[...] = with_coords(held[pl.ds(pl.multiple_of((tile ^ d) * width, width), width), :], coords[0])


def merged_pair(ours, theirs, our_coords, their_coords, pivots):
    coords = lanes(our_coords.astype(f32)[:8], their_coords.astype(f32)[:8])
    chosen = choose(coords, pivots)
    across = coords.T
    squares = None
    for f in range(coords.shape[0]):
        diff = across[:, f : f + 1] - chosen[f : f + 1, :]
        squares = diff * diff if squares is None else squares + diff * diff
    values = kernel_values(squares * (KAPPA * KAPPA))
    return dot(lanes(ours, theirs), values), chosen


def join_kernel(level, mine, got1, got2, got3, merge_pv, after, out):
    width = mine.shape[0] - 16
    _, group, _ = position()
    ours = (mine[:width, :].astype(f32) + got2[:width, :].astype(f32)).astype(bf16)
    theirs = (got1[:width, :].astype(f32) + got3[:width, :].astype(f32)).astype(bf16)
    pivots = merge_pv[level, :1, :] ^ (group * mine.shape[1])
    out[...] = with_coords(*merged_pair(ours, theirs, mine[width:, :], got1[width:, :], pivots))


def upper_half(bit):
    return lax.rem(lax.div(lax.axis_index("cluster"), 2**bit), 2)


def merge_kernel(level, bit, mine, got, merge_pv, after, out):
    width = mine.shape[0] - 16
    pivots = merge_pv[level, :1, :] ^ (upper_half(bit) * mine.shape[1])
    merged, chosen = merged_pair(mine[:width, :], got[:width, :], mine[width:, :], got[width:, :], pivots)
    ahead = merge_pv[level + 1, :1, :]
    row = lax.broadcasted_iota(jnp.int32, chosen.shape, 0)
    digits = jnp.where(row == 0, ahead & 255, jnp.where(row == 1, ahead >> 8, 0)).astype(f32)
    out[...] = jnp.concatenate([merged, chosen, digits], axis=0).astype(bf16)


def top_kernel(level, bit, mine, got1, got2, got3, merge_pv, out):
    width, rank = mine.shape[0] - 16, mine.shape[1]
    flip = upper_half(bit) * rank
    digits = got2[width:, :].astype(f32)[8:].astype(jnp.int32)
    pairs = []
    for left, right, pivots in (
        (mine, got1, merge_pv[level, :1, :]),
        (got2, got3, digits[0:1] + 256 * digits[1:2]),
    ):
        merged, chosen = merged_pair(
            left[:width, :], right[:width, :], left[width:, :], right[width:, :], pivots ^ flip
        )
        pairs.append((merged.astype(bf16), chosen))
    (ours, our_coords), (theirs, their_coords) = pairs
    pivots = merge_pv[level + 1, :1, :] ^ (upper_half(bit + 1) * rank)
    out[...] = merged_pair(ours, theirs, our_coords, their_coords, pivots)[0].astype(bf16)


def collect(ids, count, base, slots_of, boxes_of, wanted, place, pad, list_v, list_n):
    found = 0
    for v, box in zip(slots_of, boxes_of):
        used = count[box]
        for slot in range(1, ids.shape[1]):
            n = ids[box, slot] - base
            list_v[found] = v
            list_n[found] = place(n)
            found = found + ((slot < used) & wanted(n)).astype(jnp.int32)
    for i in range(3):
        list_v[found + i] = slots_of[0]
        list_n[found + i] = pad
    return found


def for_each(found, add):
    eights = lax.div(found, 8)

    def eight(i, _):
        for k in range(8):
            add(8 * i + k)
        return 0

    def four(i, _):
        for k in range(4):
            add(8 * eights + 4 * i + k)
        return 0

    lax.fori_loop(0, eights, eight, 0)
    lax.fori_loop(0, lax.div(found - 8 * eights + 3, 4), four, 0)


def far_row(right):
    row = lax.broadcasted_iota(jnp.int32, right.shape, 0)
    return jnp.where(row == 35, 1e30, 0.0).astype(bf16)


def near_own_kernel(part, ids, count, pts0, pts1, pts2, pts3, joined, *refs):
    after, out, left_ref, right_ref, list_v, list_n = refs[3 * part :]
    boxes = joined.shape[0]
    half = boxes // 2
    pair = half // 2
    cluster, group, _ = position()
    centre = centre_of(pts0[half])
    if part == 0:
        for n in range(boxes):
            right_ref[n] = features(lanes(pts0[n], pts1[n]).astype(f32), centre)[1]
        right_ref[boxes] = far_row(right_ref[0])
    mine = [part * pair + v for v in range(pair)]
    order = [group * half + v for v in mine]
    for v, box in zip(mine, order):
        whole = lanes(pts0[box], pts1[box], pts2[box], pts3[box]).astype(f32)
        left_ref[v] = features(whole, centre)[0].T.astype(bf16)

    def one(v, n):
        return dot(kernel_values(dot(left_ref[v], right_ref[n])), joined[jnp.minimum(n, boxes - 1)])

    for v, box in zip(mine, order):
        out[v] = one(v, box)
    found = collect(
        ids, count, cluster * boxes, mine, order, lambda n: (n >= 0) & (n < boxes), lambda n: n, boxes, list_v, list_n
    )

    def add(i):
        v = list_v[i]
        out[v] += one(v, list_n[i])

    for_each(found, add)


def near_halo_kernel(
    ids, count, pts0, total, left_ref, halo, after, keep, send1, send2, send3, acc, right_ref, list_v, list_n
):
    boxes, feat, rows = pts0.shape
    half = boxes // 2
    cluster, group, _ = position()
    centre = centre_of(pts0[half])
    for h in range(half):
        right_ref[h] = features(halo[h, 2 * rows :, :].astype(f32)[:feat], centre)[1]
    right_ref[half] = far_row(right_ref[0])
    order = [group * half + v for v in range(half)]
    found = collect(
        ids,
        count,
        cluster * boxes,
        range(half),
        order,
        lambda n: (n < 0) | (n >= boxes),
        lambda n: jnp.where(group == 0, n + half, n - boxes),
        half,
        list_v,
        list_n,
    )

    def add(i):
        v = list_v[i]
        h = list_n[i]
        values = kernel_values(dot(left_ref[v], right_ref[h]))
        acc[v] += dot(values, halo[jnp.minimum(h, half - 1), : 2 * rows, :])

    for_each(found, add)
    keep[...] = acc[:, :rows, :]
    for d, send in enumerate((send1, send2, send3)):
        send[...] = acc[:, (d + 1) * rows : (d + 2) * rows, :].astype(bf16)


def finish_kernel(keep, back1, back2, back3, wide, near, top):
    half = near.shape[0] // 2
    _, group, _ = position()
    near[pl.ds(group * half, half)] = (keep[...] + back2[...].astype(f32)).astype(bf16)
    near[pl.ds((1 - group) * half, half)] = (back1[...].astype(f32) + back3[...].astype(f32)).astype(bf16)
    top[0] = wide[...]


def call(body, out_shape, specs, micros, scratch=(), aliases={}):
    return pl.pallas_call(
        body,
        out_shape=out_shape,
        in_specs=specs,
        out_specs=jax.tree.map(lambda _: VMEM, out_shape),
        scratch_shapes=list(scratch),
        input_output_aliases=aliases,
        compiler_params=pltpu.CompilerParams(vmem_limit_bytes=VMEM_LIMIT),
        cost_estimate=pl.CostEstimate(flops=int(micros * 1.1e9), bytes_accessed=1024, transcendentals=0),
    )


def on_device(points, charges, near_ids, near_count, leaf_pivots, merge_pivots):
    boxes, feat, rows = points.shape
    probes = charges.shape[2]
    rank = leaf_pivots.shape[1]
    half = boxes // 2
    pair = half // 2
    tiles = lax.axis_size("tile")
    clusters = lax.axis_size("cluster")
    local_levels = boxes.bit_length() - 1

    def to_tile(x, d):
        return lax.ppermute(x, "tile", [(i, i ^ d) for i in range(tiles)])

    def to_halo(x):
        route = []
        for i in range(clusters):
            for k in range(tiles):
                target = i + 1 if k % 2 == 0 else i - 1
                if 0 <= target < clusters:
                    route.append((i * tiles + k, target * tiles + k))
        return lax.ppermute(x, ("cluster", "tile"), route)

    def partner(x, stride):
        route = [(i, i ^ stride) for i in range(clusters) if i ^ stride < clusters]
        return lax.ppermute(x, "cluster", route)

    def shape(*dims, dtype=bf16):
        return jax.ShapeDtypeStruct(dims, dtype)

    got = [to_tile(points, d) for d in range(1, 4)]
    mate = to_tile(charges, 1)
    charges = call(load_kernel, shape(*charges.shape), [VMEM], COST["load"])(charges)
    to_send, joined = call(
        stage_kernel, (shape(half, 2 * rows + 16, probes), shape(boxes, 2 * rows, probes)), [VMEM] * 4 + [ANY], COST["stage"]
    )(points, got[0], charges, mate, got[2])
    halo = to_halo(to_send)
    pts = [points] + got

    merge_pv = jnp.transpose(merge_pivots, (1, 0, 2))
    width = probes // tiles
    wide_shape = shape(width + 16, rank)
    mine, *sends = call(tree_kernel, (wide_shape,) * 4, [VMEM] * 7, COST["tree"], [pltpu.VMEM((probes, rank), f32)])(
        *pts, joined, leaf_pivots, merge_pv
    )
    others = [to_tile(sends[d - 1], d) for d in range(1, 4)]

    lists = [pltpu.SMEM((half * near_ids.shape[1] + 4,), jnp.int32)] * 2

    sums = (
        shape(half, 4 * rows, probes, dtype=f32),
        shape(half, 4 * rows, 48),
        shape(boxes + 1, 48, 2 * rows),
    )

    def near_own(part, begun, after):
        specs = [SMEM] * 2 + [VMEM] * (5 + len(begun)) + [ANY]
        aliases = {7 + i: i for i in range(len(begun))}
        return call(functools.partial(near_own_kernel, part), sums, specs, COST["own"], lists, aliases)(
            near_ids, near_count, *pts, joined, *begun, after
        )

    begun = near_own(0, [], mine)
    wide = call(functools.partial(join_kernel, local_levels - 1), wide_shape, [VMEM] * 5 + [ANY], COST["join"])(
        mine, *others, merge_pv, begun[2]
    )
    total, left, _ = near_own(1, begun, wide)
    other = partner(wide, 1)
    keep, *sends = call(
        near_halo_kernel,
        (shape(half, rows, probes, dtype=f32),) + (shape(half, rows, probes),) * 3 + sums[:1],
        [SMEM] * 2 + [VMEM] * 4 + [ANY],
        COST["halo"],
        [pltpu.VMEM((half + 1, 48, 2 * rows), bf16)] + lists,
        {3: 4},
    )(near_ids, near_count, points, total, left, halo, other)
    back = [to_tile(sends[d - 1], d) for d in range(1, 4)]

    wide = call(functools.partial(merge_kernel, local_levels, 0), wide_shape, [VMEM] * 3 + [ANY], COST["merge"])(
        wide, other, merge_pv, back[0]
    )
    top = call(functools.partial(top_kernel, local_levels + 1, 1), shape(width, rank), [VMEM] * 5, COST["merge"])(
        wide, partner(wide, 2), partner(wide, 4), partner(wide, 6), merge_pv
    )
    near, top = call(
        finish_kernel, (shape(boxes, rows, probes), shape(1, width, rank)), [VMEM] * 5, COST["finish"]
    )(keep, *back, top)
    return near, jnp.swapaxes(top, 1, 2)


def solution(mesh):
    return jax.shard_map(
        on_device,
        mesh=mesh,
        in_specs=(
            P("cluster", None, "tile"),
            P("cluster", "tile", None),
            P("cluster", None),
            P("cluster"),
            P("cluster", None),
            P("cluster", None, None),
        ),
        out_specs=(P("cluster", "tile", None), P("cluster", None, "tile")),
        check_vma=False,
    )
```

```python
import functools
import math

import jax
import jax.numpy as jnp
from jax import lax
from jax.experimental import pallas as pl
from jax.experimental.pallas import tpu as pltpu
from jax.sharding import PartitionSpec as P

SPAN = 4
lengthscale = 0.7
KAPPA = math.log2(math.e) / lengthscale
FLOOR = 1e-30
COST = dict(load=0.001, stage=0.001, tree=3, own=1, join=1, merge=1, halo=5, rest=1, finish=0.001)
VMEM_LIMIT = 16 * 1024 * 1024
f32 = jnp.float32
bf16 = jnp.bfloat16
VMEM = pl.BlockSpec(memory_space=pltpu.VMEM)
SMEM = pl.BlockSpec(memory_space=pltpu.SMEM)
ANY = pl.BlockSpec(memory_space=pl.ANY)
HBM = pl.BlockSpec(memory_space=pltpu.HBM)


def features(coords, centre):
    shifted = (coords - centre) * KAPPA
    high = shifted.astype(bf16).astype(f32)
    low = (shifted - high).astype(bf16).astype(f32)
    both = high + low
    norm = jnp.sum(both * both, axis=0, keepdims=True)
    first = norm.astype(bf16).astype(f32)
    second = (norm - first).astype(bf16).astype(f32)
    third = norm - first - second
    row = lax.broadcasted_iota(jnp.int32, coords.shape, 0)
    one = jnp.ones_like(coords)
    nil = jnp.zeros_like(coords)

    def six(a, b, c, d, e, f):
        out = jnp.where(row == 0, a, jnp.where(row == 1, b, jnp.where(row == 2, c, nil)))
        return jnp.where(row == 3, d, jnp.where(row == 4, e, jnp.where(row == 5, f, out)))

    left = [-2 * high, -2 * high, -2 * low, -2 * low, six(first, second, third, one, one, one), nil]
    right = [high, low, high, low, six(one, one, one, first, second, third), nil]
    return jnp.concatenate(left, axis=0), jnp.concatenate(right, axis=0).astype(bf16)


def kernel_values(squares):
    squares = jnp.maximum(squares, FLOOR)
    return jnp.exp2(-(squares * lax.rsqrt(squares))).astype(bf16)


def dot(a, b):
    return jnp.dot(a, b, preferred_element_type=f32)


def choose(coords, pivots):
    place = lax.broadcasted_iota(jnp.int32, (coords.shape[1], pivots.shape[1]), 0)
    return dot(coords.astype(bf16), jnp.where(place == pivots, 1.0, 0.0).astype(bf16))


def lanes(*parts):
    return jnp.concatenate(parts, axis=1)


def centre_of(coords):
    return jnp.mean(coords.astype(f32), axis=1, keepdims=True)


def position():
    tile = lax.axis_index("tile")
    return lax.axis_index("cluster"), lax.rem(tile, 2), tile


def load_kernel(*refs):
    count = len(refs) // 2
    for copy in start_copies(list(zip(refs[:count], refs[count:])), refs[-1]):
        copy.wait()


def stage_kernel(points, got1, charges, mate, after, to_send, joined):
    boxes, feat, rows = got1.shape
    joined[:, :rows, :] = charges[...]
    joined[:, rows:, :] = mate[...]
    count = boxes // 2
    start = jnp.where(position()[1] == 0, boxes - count, 0)
    coords = []
    for i in range(count):
        box = start + i
        to_send[2 * i * rows : (2 * i + 1) * rows, :] = charges[box]
        to_send[(2 * i + 1) * rows : 2 * (i + 1) * rows, :] = mate[box]
        coords.append(lanes(points[box], got1[box]).astype(f32))
    to_send[2 * count * rows :, :] = jnp.concatenate(coords, axis=0).astype(bf16)


def with_coords(weights, coords):
    return jnp.concatenate([weights, coords, jnp.zeros_like(coords)], axis=0).astype(bf16)


def tree_kernel(pts0, pts1, pts2, pts3, joined, leaf_pv, merge_pv, *refs):
    outs, held = refs[:4], refs[4]
    half = leaf_pv.shape[0] // 2
    rows = pts0.shape[2]
    _, group, tile = position()
    centre = centre_of(pts0[half])
    coords, weights = [], []
    for i in range(half):
        box = group * half + i
        whole = lanes(pts0[box], pts1[box], pts2[box], pts3[box]).astype(f32)
        chosen = choose(whole, leaf_pv[pl.ds(box, 1), :] ^ (tile * rows))
        left, _ = features(chosen, centre)
        _, right = features(whole[:, : 2 * rows], centre)
        values = kernel_values(dot(left.T.astype(bf16), right))
        coords.append(chosen)
        weights.append(dot(values, joined[box]))
    level = 0
    while len(coords) > 1:
        next_coords, next_weights = [], []
        for i in range(len(coords) // 2):
            cand = lanes(coords[2 * i], coords[2 * i + 1])
            pair = group * (half // 2) + i * 2**level
            chosen = choose(cand, merge_pv[level, pl.ds(pair, 1), :])
            left, _ = features(chosen, centre)
            _, right = features(cand, centre)
            values = kernel_values(dot(left.T.astype(bf16), right))
            charge = jnp.concatenate([weights[2 * i], weights[2 * i + 1]], axis=0).astype(bf16)
            next_coords.append(chosen)
            next_weights.append(dot(values, charge))
        coords, weights = next_coords, next_weights
        level += 1
    held[...] = weights[0].T
    width = held.shape[0] // 4
    for d, out in enumerate(outs):
        out[...] = with_coords(held[pl.ds(pl.multiple_of((tile ^ d) * width, width), width), :], coords[0])


def merged_pair(ours, theirs, our_coords, their_coords, pivots, near=False):
    coords = lanes(our_coords.astype(f32)[:8], their_coords.astype(f32)[:8])
    chosen = choose(coords, pivots)
    if near:
        centre = centre_of(coords)
        left, right = features(coords, centre)[0], features(chosen, centre)[1]
        return dot(lanes(ours, theirs), kernel_values(dot(left.T.astype(bf16), right))), chosen
    across = coords.T
    squares = None
    for f in range(coords.shape[0]):
        diff = across[:, f : f + 1] - chosen[f : f + 1, :]
        squares = diff * diff if squares is None else squares + diff * diff
    values = kernel_values(squares * (KAPPA * KAPPA))
    return dot(lanes(ours, theirs), values), chosen


def join_kernel(level, mine, got1, got2, got3, merge_pv, after, out):
    width = mine.shape[0] - 16
    _, group, _ = position()
    ours = (mine[:width, :].astype(f32) + got2[:width, :].astype(f32)).astype(bf16)
    theirs = (got1[:width, :].astype(f32) + got3[:width, :].astype(f32)).astype(bf16)
    pivots = merge_pv[level, :1, :] ^ (group * mine.shape[1])
    out[...] = with_coords(*merged_pair(ours, theirs, mine[width:, :], got1[width:, :], pivots, True))


def upper_half(bit):
    return lax.rem(lax.div(lax.axis_index("cluster"), 2**bit), 2)


def merge_kernel(level, bit, mine, got, merge_pv, after, out):
    width = mine.shape[0] - 16
    pivots = merge_pv[level, :1, :] ^ (upper_half(bit) * mine.shape[1])
    merged, chosen = merged_pair(mine[:width, :], got[:width, :], mine[width:, :], got[width:, :], pivots)
    ahead = merge_pv[level + 1, :1, :]
    row = lax.broadcasted_iota(jnp.int32, chosen.shape, 0)
    digits = jnp.where(row == 0, ahead & 255, jnp.where(row == 1, ahead >> 8, 0)).astype(f32)
    out[...] = jnp.concatenate([merged, chosen, digits], axis=0).astype(bf16)


def top_kernel(level, bit, mine, got1, got2, got3, merge_pv, out):
    width, rank = mine.shape[0] - 16, mine.shape[1]
    flip = upper_half(bit) * rank
    digits = got2[width:, :].astype(f32)[8:].astype(jnp.int32)
    pairs = []
    for left, right, pivots in (
        (mine, got1, merge_pv[level, :1, :]),
        (got2, got3, digits[0:1] + 256 * digits[1:2]),
    ):
        merged, chosen = merged_pair(
            left[:width, :], right[:width, :], left[width:, :], right[width:, :], pivots ^ flip
        )
        pairs.append((merged.astype(bf16), chosen))
    (ours, our_coords), (theirs, their_coords) = pairs
    pivots = merge_pv[level + 1, :1, :] ^ (upper_half(bit + 1) * rank)
    out[...] = merged_pair(ours, theirs, our_coords, their_coords, pivots)[0].astype(bf16)


def start_copies(pairs, sem):
    copies = [pltpu.make_async_copy(one, other, sem.at[i]) for i, (one, other) in enumerate(pairs)]
    for copy in copies:
        copy.start()
    return copies


def collect(ids, count, base, slots_of, boxes_of, wanted, place, pad, list_v, list_n):
    found = 0
    for v, box in zip(slots_of, boxes_of):
        used = count[box]
        for slot in range(1, ids.shape[1]):
            n = ids[box, slot] - base
            list_v[found] = v
            list_n[found] = place(n)
            found = found + ((slot < used) & wanted(n)).astype(jnp.int32)
    for i in range(3):
        list_v[found + i] = slots_of[0]
        list_n[found + i] = pad
    return found


def for_each(found, add):
    eights = lax.div(found, 8)
    rest = found - 8 * eights
    fours = lax.div(rest + 1, 4)
    twos = lax.div(rest - 4 * fours + 1, 2)

    def run(first, steps, size):
        def step(i, _):
            for k in range(size):
                add(first + size * i + k)
            return 0

        lax.fori_loop(0, steps, step, 0)

    run(0, eights, 8)
    run(8 * eights, fours, 4)
    run(8 * eights + 4 * fours, twos, 2)


def far_row(right):
    row = lax.broadcasted_iota(jnp.int32, right.shape, 0)
    return jnp.where(row == 35, 1e30, 0.0).astype(bf16)


def near_own_kernel(part, all_ids, all_counts, pts0, pts1, pts2, pts3, joined, *refs):
    after, out, left_ref, right_ref, list_v, list_n, ids, count, sem = refs[3 * part :]
    copies = start_copies([(all_ids, ids), (all_counts, count)], sem)
    boxes = joined.shape[0]
    half = boxes // 2
    pair = half // 2
    cluster, group, _ = position()
    centre = centre_of(pts0[half])
    if part == 0:
        for n in range(boxes):
            right_ref[n] = features(lanes(pts0[n], pts1[n]).astype(f32), centre)[1]
        right_ref[boxes] = far_row(right_ref[0])
    mine = [part * pair + v for v in range(pair)]
    order = [group * half + v for v in mine]
    for v, box in zip(mine, order):
        whole = lanes(pts0[box], pts1[box], pts2[box], pts3[box]).astype(f32)
        left_ref[v] = features(whole, centre)[0].T.astype(bf16)

    def one(v, n):
        return dot(kernel_values(dot(left_ref[v], right_ref[n])), joined[jnp.minimum(n, boxes - 1)])

    for v, box in zip(mine, order):
        out[v] = one(v, box)
    for copy in copies:
        copy.wait()
    found = collect(
        ids, count, cluster * boxes, mine, order, lambda n: (n >= 0) & (n < boxes), lambda n: n, boxes, list_v, list_n
    )

    def add(i):
        v = list_v[i]
        out[v] += one(v, list_n[i])

    for_each(found, add)


def near_halo_kernel(part, all_ids, all_counts, pts0, total, left_ref, halo, after, *refs):
    if part == 0:
        send1, send2, send3, acc, right_ref, list_v, list_n, ids, count, sem = refs
    else:
        right_ref, keep, acc, list_v, list_n, ids, count, sem = refs
    copies = start_copies([(all_ids, ids), (all_counts, count)], sem)
    boxes, feat, rows = pts0.shape
    half = boxes // 2
    cluster, group, _ = position()
    if part == 0:
        centre = centre_of(pts0[half])
        coords = halo[2 * half * rows :, :].astype(f32)
        for h in range(half):
            right_ref[h] = features(coords[h * feat : (h + 1) * feat], centre)[1]
        right_ref[half] = far_row(right_ref[0])
    order = [group * half + v for v in range(half)]
    for copy in copies:
        copy.wait()
    found = collect(
        ids,
        count,
        cluster * boxes,
        range(half),
        order,
        lambda n: (n < 0) | (n >= boxes),
        lambda n: jnp.where(group == 0, n + half, n - boxes),
        half,
        list_v,
        list_n,
    )
    mine = slice(0, rows) if part else slice(rows, 4 * rows)

    def add(i):
        v = list_v[i]
        h = list_n[i]
        values = kernel_values(dot(left_ref[v, mine, :], right_ref[h]))
        start = pl.multiple_of(jnp.minimum(h, half - 1) * (2 * rows), 2 * rows)
        acc[v, mine, :] += dot(values, halo[pl.ds(start, 2 * rows), :])

    for_each(found, add)
    if part == 0:
        for d, send in enumerate((send1, send2, send3)):
            send[...] = acc[:, (d + 1) * rows : (d + 2) * rows, :].astype(bf16)
    else:
        keep[...] = acc[:, :rows, :]


def finish_kernel(keep, back1, back2, back3, wide, near, top, held, sem, top_sem):
    half = held.shape[0] // 2
    _, group, _ = position()
    copies = [pltpu.make_async_copy(wide, top.at[0], top_sem)]
    copies[0].start()
    for side, (one, two) in enumerate(((keep, back2), (back1, back3))):
        for i in range(half):
            j = side * half + i
            held[j] = (one[i].astype(f32) + two[i].astype(f32)).astype(bf16)
            copies.append(pltpu.make_async_copy(held.at[j], near.at[(group ^ side) * half + i], sem.at[j]))
            copies[-1].start()
    for copy in copies:
        copy.wait()


def call(body, out_shape, specs, micros, scratch=(), aliases={}, out_spec=VMEM):
    return pl.pallas_call(
        body,
        out_shape=out_shape,
        in_specs=specs,
        out_specs=jax.tree.map(lambda _: out_spec, out_shape),
        scratch_shapes=list(scratch),
        input_output_aliases=aliases,
        compiler_params=pltpu.CompilerParams(vmem_limit_bytes=VMEM_LIMIT),
        cost_estimate=pl.CostEstimate(flops=int(micros * 1.1e9), bytes_accessed=1024, transcendentals=0),
    )


def on_device(points, charges, near_ids, near_count, leaf_pivots, merge_pivots):
    boxes, feat, rows = points.shape
    probes = charges.shape[2]
    rank = leaf_pivots.shape[1]
    half = boxes // 2
    pair = half // 2
    tiles = lax.axis_size("tile")
    clusters = lax.axis_size("cluster")
    local_levels = boxes.bit_length() - 1

    def to_tile(x, d):
        return lax.ppermute(x, "tile", [(i, i ^ d) for i in range(tiles)])

    def to_halo(x):
        route = []
        for i in range(clusters):
            for k in range(tiles):
                target = i + 1 if k % 2 == 0 else i - 1
                if 0 <= target < clusters:
                    route.append((i * tiles + k, target * tiles + k))
        return lax.ppermute(x, ("cluster", "tile"), route)

    def partner(x, stride):
        route = [(i, i ^ stride) for i in range(clusters) if i ^ stride < clusters]
        return lax.ppermute(x, "cluster", route)

    def shape(*dims, dtype=bf16):
        return jax.ShapeDtypeStruct(dims, dtype)

    got = [to_tile(points, d) for d in range(1, 4)]
    mate = to_tile(charges, 1)
    merge_pv = jnp.transpose(merge_pivots, (1, 0, 2))
    arguments = [points, charges, leaf_pivots, merge_pv, near_ids, near_count]
    points, charges, leaf_pv, merge_pv, near_ids, near_count = call(
        load_kernel,
        tuple(jax.ShapeDtypeStruct(x.shape, x.dtype) for x in arguments),
        [HBM] * len(arguments),
        COST["load"],
        [pltpu.SemaphoreType.DMA((len(arguments),))],
    )(*[pltpu.with_memory_space_constraint(x, pltpu.HBM) for x in arguments])
    to_send, joined = call(
        stage_kernel, (shape(half * (2 * rows + feat), probes), shape(boxes, 2 * rows, probes)), [VMEM] * 4 + [ANY], COST["stage"]
    )(points, got[0], charges, mate, got[2])
    halo = to_halo(to_send)
    pts = [points] + got

    width = probes // tiles
    wide_shape = shape(width + 16, rank)
    mine, *sends = call(tree_kernel, (wide_shape,) * 4, [VMEM] * 7, COST["tree"], [pltpu.VMEM((probes, rank), f32)])(
        *pts, joined, leaf_pv, merge_pv
    )
    others = [to_tile(sends[d - 1], d) for d in range(1, 4)]

    lists = [pltpu.SMEM((half * near_ids.shape[1] + 4,), jnp.int32)] * 2
    lists += [pltpu.SMEM(x.shape, jnp.int32) for x in (near_ids, near_count)] + [pltpu.SemaphoreType.DMA((2,))]

    sums = (
        shape(half, 4 * rows, probes, dtype=f32),
        shape(half, 4 * rows, 48),
        shape(boxes + 1, 48, 2 * rows),
    )

    def near_own(part, begun, after):
        specs = [ANY] * 2 + [VMEM] * (5 + len(begun)) + [ANY]
        aliases = {7 + i: i for i in range(len(begun))}
        return call(functools.partial(near_own_kernel, part), sums, specs, COST["own"], lists, aliases)(
            near_ids, near_count, *pts, joined, *begun, after
        )

    begun = near_own(0, [], mine)
    wide = call(functools.partial(join_kernel, local_levels - 1), wide_shape, [VMEM] * 5 + [ANY], COST["join"])(
        mine, *others, merge_pv, begun[2]
    )
    total, left, _ = near_own(1, begun, wide)
    other = partner(wide, 1)
    quarter = shape(half, rows, probes)
    inputs = (near_ids, near_count, points)
    *sends, total, right = call(
        functools.partial(near_halo_kernel, 0),
        (quarter, quarter, quarter, sums[0], shape(half + 1, 48, 2 * rows)),
        [ANY] * 2 + [VMEM] * 4 + [ANY],
        COST["halo"],
        lists,
        {3: 3},
    )(*inputs, total, left, halo, other)
    back = [to_tile(sends[d - 1], d) for d in range(1, 4)]
    keep, _ = call(
        functools.partial(near_halo_kernel, 1),
        (shape(half, rows, probes, dtype=f32), sums[0]),
        [ANY] * 2 + [VMEM] * 4 + [ANY, VMEM],
        COST["rest"],
        lists,
        {3: 1},
    )(*inputs, total, left, halo, back[0], right)

    wide = call(functools.partial(merge_kernel, local_levels, 0), wide_shape, [VMEM] * 3 + [ANY], COST["merge"])(
        wide, other, merge_pv, back[0]
    )
    top = call(functools.partial(top_kernel, local_levels + 1, 1), shape(width, rank), [VMEM] * 5, COST["merge"])(
        wide, partner(wide, 2), partner(wide, 4), partner(wide, 6), merge_pv
    )
    near, top = call(
        finish_kernel,
        (shape(boxes, rows, probes), shape(1, width, rank)),
        [VMEM] * 5,
        COST["finish"],
        [pltpu.VMEM((boxes, rows, probes), bf16), pltpu.SemaphoreType.DMA((boxes,)), pltpu.SemaphoreType.DMA],
        {},
        HBM,
    )(keep, *back, top)
    return near, jnp.swapaxes(top, 1, 2)


def solution(mesh):
    return jax.shard_map(
        on_device,
        mesh=mesh,
        in_specs=(
            P("cluster", None, "tile"),
            P("cluster", "tile", None),
            P("cluster", None),
            P("cluster"),
            P("cluster", None),
            P("cluster", None, None),
        ),
        out_specs=(P("cluster", "tile", None), P("cluster", None, "tile")),
        check_vma=False,
    )
```

```python
import functools
import math

import jax
import jax.numpy as jnp
from jax import lax
from jax.experimental import pallas as pl
from jax.experimental.pallas import tpu as pltpu
from jax.sharding import PartitionSpec as P

SPAN = 4
lengthscale = 0.7
KAPPA = math.log2(math.e) / lengthscale
FLOOR = 1e-30
COST = dict(load=0.001, stage=0.001, tree=3, own=1, join=1, merge=5, halo=5, rest=1, top=0.001, finish=0.001)
VMEM_LIMIT = 16 * 1024 * 1024
f32 = jnp.float32
bf16 = jnp.bfloat16
VMEM = pl.BlockSpec(memory_space=pltpu.VMEM)
SMEM = pl.BlockSpec(memory_space=pltpu.SMEM)
ANY = pl.BlockSpec(memory_space=pl.ANY)
HBM = pl.BlockSpec(memory_space=pltpu.HBM)


def features(coords, centre):
    shifted = (coords - centre) * KAPPA
    high = shifted.astype(bf16).astype(f32)
    low = (shifted - high).astype(bf16).astype(f32)
    both = high + low
    norm = jnp.sum(both * both, axis=0, keepdims=True)
    first = norm.astype(bf16).astype(f32)
    second = (norm - first).astype(bf16).astype(f32)
    third = norm - first - second
    row = lax.broadcasted_iota(jnp.int32, coords.shape, 0)
    one = jnp.ones_like(coords)
    nil = jnp.zeros_like(coords)

    def six(a, b, c, d, e, f):
        out = jnp.where(row == 0, a, jnp.where(row == 1, b, jnp.where(row == 2, c, nil)))
        return jnp.where(row == 3, d, jnp.where(row == 4, e, jnp.where(row == 5, f, out)))

    left = [-2 * high, -2 * high, -2 * low, -2 * low, six(first, second, third, one, one, one), nil]
    right = [high, low, high, low, six(one, one, one, first, second, third), nil]
    return jnp.concatenate(left, axis=0), jnp.concatenate(right, axis=0).astype(bf16)


def kernel_values(squares):
    squares = jnp.maximum(squares, FLOOR)
    return jnp.exp2(-(squares * lax.rsqrt(squares))).astype(bf16)


def dot(a, b):
    return jnp.dot(a, b, preferred_element_type=f32)


def choose(coords, pivots):
    place = lax.broadcasted_iota(jnp.int32, (coords.shape[1], pivots.shape[1]), 0)
    return dot(coords.astype(bf16), jnp.where(place == pivots, 1.0, 0.0).astype(bf16))


def lanes(*parts):
    return jnp.concatenate(parts, axis=1)


def centre_of(coords):
    return jnp.mean(coords.astype(f32), axis=1, keepdims=True)


def position():
    tile = lax.axis_index("tile")
    return lax.axis_index("cluster"), lax.rem(tile, 2), tile


def load_kernel(*refs):
    count = len(refs) // 2
    for copy in start_copies(list(zip(refs[:count], refs[count:])), refs[-1]):
        copy.wait()


def stage_kernel(points, got1, charges, mate, after, to_send, joined):
    boxes, feat, rows = got1.shape
    joined[:, :rows, :] = charges[...]
    joined[:, rows:, :] = mate[...]
    count = boxes // 2
    start = jnp.where(position()[1] == 0, boxes - count, 0)
    coords = []
    for i in range(count):
        box = start + i
        to_send[2 * i * rows : (2 * i + 1) * rows, :] = charges[box]
        to_send[(2 * i + 1) * rows : 2 * (i + 1) * rows, :] = mate[box]
        coords.append(lanes(points[box], got1[box]).astype(f32))
    to_send[2 * count * rows :, :] = jnp.concatenate(coords, axis=0).astype(bf16)


def with_coords(weights, coords):
    return jnp.concatenate([weights, coords, jnp.zeros_like(coords)], axis=0).astype(bf16)


def tree_kernel(pts0, pts1, pts2, pts3, joined, leaf_pv, merge_pv, *refs):
    outs, held = refs[:4], refs[4]
    half = leaf_pv.shape[0] // 2
    rows = pts0.shape[2]
    _, group, tile = position()
    centre = centre_of(pts0[half])
    coords, weights = [], []
    for i in range(half):
        box = group * half + i
        whole = lanes(pts0[box], pts1[box], pts2[box], pts3[box]).astype(f32)
        chosen = choose(whole, leaf_pv[pl.ds(box, 1), :] ^ (tile * rows))
        left, _ = features(chosen, centre)
        _, right = features(whole[:, : 2 * rows], centre)
        values = kernel_values(dot(left.T.astype(bf16), right))
        coords.append(chosen)
        weights.append(dot(values, joined[box]))
    level = 0
    while len(coords) > 1:
        next_coords, next_weights = [], []
        for i in range(len(coords) // 2):
            cand = lanes(coords[2 * i], coords[2 * i + 1])
            pair = group * (half // 2) + i * 2**level
            chosen = choose(cand, merge_pv[level, pl.ds(pair, 1), :])
            left, _ = features(chosen, centre)
            _, right = features(cand, centre)
            values = kernel_values(dot(left.T.astype(bf16), right))
            charge = jnp.concatenate([weights[2 * i], weights[2 * i + 1]], axis=0).astype(bf16)
            next_coords.append(chosen)
            next_weights.append(dot(values, charge))
        coords, weights = next_coords, next_weights
        level += 1
    held[...] = weights[0].T
    width = held.shape[0] // 4
    for d, out in enumerate(outs):
        out[...] = with_coords(held[pl.ds(pl.multiple_of((tile ^ d) * width, width), width), :], coords[0])


def merged_pair(ours, theirs, our_coords, their_coords, pivots, near=False):
    coords = lanes(our_coords.astype(f32)[:8], their_coords.astype(f32)[:8])
    chosen = choose(coords, pivots)
    if near:
        centre = centre_of(coords)
        left, right = features(coords, centre)[0], features(chosen, centre)[1]
        return dot(lanes(ours, theirs), kernel_values(dot(left.T.astype(bf16), right))), chosen
    across = coords.T
    squares = None
    for f in range(coords.shape[0]):
        diff = across[:, f : f + 1] - chosen[f : f + 1, :]
        squares = diff * diff if squares is None else squares + diff * diff
    values = kernel_values(squares * (KAPPA * KAPPA))
    return dot(lanes(ours, theirs), values), chosen


def join_kernel(level, mine, got1, got2, got3, merge_pv, after, out):
    width = mine.shape[0] - 16
    _, group, _ = position()
    ours = (mine[:width, :].astype(f32) + got2[:width, :].astype(f32)).astype(bf16)
    theirs = (got1[:width, :].astype(f32) + got3[:width, :].astype(f32)).astype(bf16)
    pivots = merge_pv[level, :1, :] ^ (group * mine.shape[1])
    out[...] = with_coords(*merged_pair(ours, theirs, mine[width:, :], got1[width:, :], pivots, True))


def upper_half(bit):
    return lax.rem(lax.div(lax.axis_index("cluster"), 2**bit), 2)


def merge_kernel(level, bit, mine, got, merge_pv, after, out):
    width = mine.shape[0] - 16
    pivots = merge_pv[level, :1, :] ^ (upper_half(bit) * mine.shape[1])
    merged, chosen = merged_pair(mine[:width, :], got[:width, :], mine[width:, :], got[width:, :], pivots)
    ahead = merge_pv[level + 1, :1, :]
    row = lax.broadcasted_iota(jnp.int32, chosen.shape, 0)
    digits = jnp.where(row == 0, ahead & 255, jnp.where(row == 1, ahead >> 8, 0)).astype(f32)
    out[...] = jnp.concatenate([merged, chosen, digits], axis=0).astype(bf16)


def top_kernel(level, bit, mine, got1, got2, got3, merge_pv, out):
    width, rank = mine.shape[0] - 16, mine.shape[1]
    flip = upper_half(bit) * rank
    digits = got2[width:, :].astype(f32)[8:].astype(jnp.int32)
    pairs = []
    for left, right, pivots in (
        (mine, got1, merge_pv[level, :1, :]),
        (got2, got3, digits[0:1] + 256 * digits[1:2]),
    ):
        merged, chosen = merged_pair(
            left[:width, :], right[:width, :], left[width:, :], right[width:, :], pivots ^ flip
        )
        pairs.append((merged.astype(bf16), chosen))
    (ours, our_coords), (theirs, their_coords) = pairs
    pivots = merge_pv[level + 1, :1, :] ^ (upper_half(bit + 1) * rank)
    out[...] = merged_pair(ours, theirs, our_coords, their_coords, pivots)[0].astype(bf16)


def start_copies(pairs, sem):
    copies = [pltpu.make_async_copy(one, other, sem.at[i]) for i, (one, other) in enumerate(pairs)]
    for copy in copies:
        copy.start()
    return copies


def collect(ids, count, base, slots_of, boxes_of, wanted, place, pad, list_v, list_n):
    found = 0
    for v, box in zip(slots_of, boxes_of):
        used = count[box]
        for slot in range(1, ids.shape[1]):
            n = ids[box, slot] - base
            list_v[found] = v
            list_n[found] = place(n)
            found = found + ((slot < used) & wanted(n)).astype(jnp.int32)
    for i in range(3):
        list_v[found + i] = slots_of[0]
        list_n[found + i] = pad
    return found


def for_each(found, add):
    eights = lax.div(found, 8)
    rest = found - 8 * eights
    fours = lax.div(rest + 1, 4)
    twos = lax.div(rest - 4 * fours + 1, 2)

    def run(first, steps, size):
        def step(i, _):
            for k in range(size):
                add(first + size * i + k)
            return 0

        lax.fori_loop(0, steps, step, 0)

    run(0, eights, 8)
    run(8 * eights, fours, 4)
    run(8 * eights + 4 * fours, twos, 2)


def far_row(right):
    row = lax.broadcasted_iota(jnp.int32, right.shape, 0)
    return jnp.where(row == 35, 1e30, 0.0).astype(bf16)


def near_own_kernel(part, all_ids, all_counts, pts0, pts1, pts2, pts3, joined, *refs):
    after, out, left_ref, right_ref, list_v, list_n, ids, count, sem = refs[3 * part :]
    copies = start_copies([(all_ids, ids), (all_counts, count)], sem)
    boxes = joined.shape[0]
    half = boxes // 2
    pair = half // 2
    cluster, group, _ = position()
    centre = centre_of(pts0[half])
    if part == 0:
        for n in range(boxes):
            right_ref[n] = features(lanes(pts0[n], pts1[n]).astype(f32), centre)[1]
        right_ref[boxes] = far_row(right_ref[0])
    mine = [part * pair + v for v in range(pair)]
    order = [group * half + v for v in mine]
    for v, box in zip(mine, order):
        whole = lanes(pts0[box], pts1[box], pts2[box], pts3[box]).astype(f32)
        left_ref[v] = features(whole, centre)[0].T.astype(bf16)

    def one(v, n):
        return dot(kernel_values(dot(left_ref[v], right_ref[n])), joined[jnp.minimum(n, boxes - 1)])

    for v, box in zip(mine, order):
        out[v] = one(v, box)
    for copy in copies:
        copy.wait()
    found = collect(
        ids, count, cluster * boxes, mine, order, lambda n: (n >= 0) & (n < boxes), lambda n: n, boxes, list_v, list_n
    )

    def add(i):
        v = list_v[i]
        out[v] += one(v, list_n[i])

    for_each(found, add)


def near_halo_kernel(part, all_ids, all_counts, pts0, total, left_ref, halo, after, *refs):
    if part == 0:
        send1, send2, send3, acc, right_ref, mark, list_v, list_n, ids, count, sem = refs
    else:
        right_ref, keep, acc, list_v, list_n, ids, count, sem = refs
    copies = start_copies([(all_ids, ids), (all_counts, count)], sem)
    boxes, feat, rows = pts0.shape
    half = boxes // 2
    cluster, group, _ = position()
    if part == 0:
        centre = centre_of(pts0[half])
        coords = halo[2 * half * rows :, :].astype(f32)
        for h in range(half):
            right_ref[h] = features(coords[h * feat : (h + 1) * feat], centre)[1]
        right_ref[half] = far_row(right_ref[0])
    order = [group * half + v for v in range(half)]
    for copy in copies:
        copy.wait()
    found = collect(
        ids,
        count,
        cluster * boxes,
        range(half),
        order,
        lambda n: (n < 0) | (n >= boxes),
        lambda n: jnp.where(group == 0, n + half, n - boxes),
        half,
        list_v,
        list_n,
    )
    mine = slice(0, rows) if part else slice(rows, 4 * rows)

    def add(i):
        v = list_v[i]
        h = list_n[i]
        values = kernel_values(dot(left_ref[v, mine, :], right_ref[h]))
        start = pl.multiple_of(jnp.minimum(h, half - 1) * (2 * rows), 2 * rows)
        acc[v, mine, :] += dot(values, halo[pl.ds(start, 2 * rows), :])

    for_each(found, add)
    if part == 0:
        mark[...] = jnp.zeros_like(mark)
        for d, send in enumerate((send1, send2, send3)):
            send[...] = acc[:, (d + 1) * rows : (d + 2) * rows, :].astype(bf16)
    else:
        keep[...] = acc[:, :rows, :]


def pass_kernel(given, after, out):
    out[...] = given[...]


def finish_kernel(keep, back1, back2, back3, wide, near, top, held, sem, top_sem):
    half = held.shape[0] // 2
    _, group, _ = position()
    copies = [pltpu.make_async_copy(wide, top.at[0], top_sem)]
    copies[0].start()
    for side, (one, two) in enumerate(((keep, back2), (back1, back3))):
        for i in range(half):
            j = side * half + i
            held[j] = (one[i].astype(f32) + two[i].astype(f32)).astype(bf16)
            copies.append(pltpu.make_async_copy(held.at[j], near.at[(group ^ side) * half + i], sem.at[j]))
            copies[-1].start()
    for copy in copies:
        copy.wait()


def call(body, out_shape, specs, micros, scratch=(), aliases={}, out_spec=VMEM):
    return pl.pallas_call(
        body,
        out_shape=out_shape,
        in_specs=specs,
        out_specs=jax.tree.map(lambda _: out_spec, out_shape),
        scratch_shapes=list(scratch),
        input_output_aliases=aliases,
        compiler_params=pltpu.CompilerParams(vmem_limit_bytes=VMEM_LIMIT),
        cost_estimate=pl.CostEstimate(flops=int(micros * 1.1e9), bytes_accessed=1024, transcendentals=0),
    )


def on_device(points, charges, near_ids, near_count, leaf_pivots, merge_pivots):
    boxes, feat, rows = points.shape
    probes = charges.shape[2]
    rank = leaf_pivots.shape[1]
    half = boxes // 2
    pair = half // 2
    tiles = lax.axis_size("tile")
    clusters = lax.axis_size("cluster")
    local_levels = boxes.bit_length() - 1

    def to_tile(x, d):
        return lax.ppermute(x, "tile", [(i, i ^ d) for i in range(tiles)])

    def to_halo(x):
        route = []
        for i in range(clusters):
            for k in range(tiles):
                target = i + 1 if k % 2 == 0 else i - 1
                if 0 <= target < clusters:
                    route.append((i * tiles + k, target * tiles + k))
        return lax.ppermute(x, ("cluster", "tile"), route)

    def partner(x, stride):
        route = [(i, i ^ stride) for i in range(clusters) if i ^ stride < clusters]
        return lax.ppermute(x, "cluster", route)

    def shape(*dims, dtype=bf16):
        return jax.ShapeDtypeStruct(dims, dtype)

    got = [to_tile(points, d) for d in range(1, 4)]
    mate = to_tile(charges, 1)
    merge_pv = jnp.transpose(merge_pivots, (1, 0, 2))
    arguments = [points, charges, leaf_pivots, merge_pv, near_ids, near_count]
    points, charges, leaf_pv, merge_pv, near_ids, near_count = call(
        load_kernel,
        tuple(jax.ShapeDtypeStruct(x.shape, x.dtype) for x in arguments),
        [HBM] * len(arguments),
        COST["load"],
        [pltpu.SemaphoreType.DMA((len(arguments),))],
    )(*[pltpu.with_memory_space_constraint(x, pltpu.HBM) for x in arguments])
    to_send, joined = call(
        stage_kernel, (shape(half * (2 * rows + feat), probes), shape(boxes, 2 * rows, probes)), [VMEM] * 4 + [ANY], COST["stage"]
    )(points, got[0], charges, mate, got[2])
    halo = to_halo(to_send)
    pts = [points] + got

    width = probes // tiles
    wide_shape = shape(width + 16, rank)
    mine, *sends = call(tree_kernel, (wide_shape,) * 4, [VMEM] * 7, COST["tree"], [pltpu.VMEM((probes, rank), f32)])(
        *pts, joined, leaf_pv, merge_pv
    )
    others = [to_tile(sends[d - 1], d) for d in range(1, 4)]

    lists = [pltpu.SMEM((half * near_ids.shape[1] + 4,), jnp.int32)] * 2
    lists += [pltpu.SMEM(x.shape, jnp.int32) for x in (near_ids, near_count)] + [pltpu.SemaphoreType.DMA((2,))]

    sums = (
        shape(half, 4 * rows, probes, dtype=f32),
        shape(half, 4 * rows, 48),
        shape(boxes + 1, 48, 2 * rows),
    )

    def near_own(part, begun, after):
        specs = [ANY] * 2 + [VMEM] * (5 + len(begun)) + [ANY]
        aliases = {7 + i: i for i in range(len(begun))}
        return call(functools.partial(near_own_kernel, part), sums, specs, COST["own"], lists, aliases)(
            near_ids, near_count, *pts, joined, *begun, after
        )

    begun = near_own(0, [], mine)
    wide = call(functools.partial(join_kernel, local_levels - 1), wide_shape, [VMEM] * 5 + [ANY], COST["join"])(
        mine, *others, merge_pv, begun[2]
    )
    total, left, _ = near_own(1, begun, wide)
    other = partner(wide, 1)
    quarter = shape(half, rows, probes)
    inputs = (near_ids, near_count, points)
    *sends, total, right, mark = call(
        functools.partial(near_halo_kernel, 0),
        (quarter, quarter, quarter, sums[0], shape(half + 1, 48, 2 * rows), shape(16, 128)),
        [ANY] * 2 + [VMEM] * 4 + [ANY],
        COST["halo"],
        lists,
        {3: 3},
    )(*inputs, total, left, halo, left)
    back2, back3, back1 = [to_tile(sends[d - 1], d) for d in (2, 3, 1)]
    back = [back1, back2, back3]
    keep, _ = call(
        functools.partial(near_halo_kernel, 1),
        (shape(half, rows, probes, dtype=f32), sums[0]),
        [ANY] * 2 + [VMEM] * 4 + [ANY, VMEM],
        COST["rest"],
        lists,
        {3: 1},
    )(*inputs, total, left, halo, back[0], right)

    wide = call(functools.partial(merge_kernel, local_levels, 0), wide_shape, [VMEM] * 3 + [ANY], COST["merge"])(
        wide, other, merge_pv, to_tile(mark, 1)
    )
    wide = call(pass_kernel, wide_shape, [VMEM, ANY], COST["load"])(wide, back[0])
    top = call(functools.partial(top_kernel, local_levels + 1, 1), shape(width, rank), [VMEM] * 5, COST["top"])(
        wide, partner(wide, 2), partner(wide, 4), partner(wide, 6), merge_pv
    )
    near, top = call(
        finish_kernel,
        (shape(boxes, rows, probes), shape(1, width, rank)),
        [VMEM] * 5,
        COST["finish"],
        [pltpu.VMEM((boxes, rows, probes), bf16), pltpu.SemaphoreType.DMA((boxes,)), pltpu.SemaphoreType.DMA],
        {},
        HBM,
    )(keep, *back, top)
    return near, jnp.swapaxes(top, 1, 2)


def solution(mesh):
    return jax.shard_map(
        on_device,
        mesh=mesh,
        in_specs=(
            P("cluster", None, "tile"),
            P("cluster", "tile", None),
            P("cluster", None),
            P("cluster"),
            P("cluster", None),
            P("cluster", None, None),
        ),
        out_specs=(P("cluster", "tile", None), P("cluster", None, "tile")),
        check_vma=False,
    )
```

```python
import functools
import math

import jax
import jax.numpy as jnp
from jax import lax
from jax.experimental import pallas as pl
from jax.experimental.pallas import tpu as pltpu
from jax.sharding import PartitionSpec as P

SPAN = 4
lengthscale = 0.7
KAPPA = math.log2(math.e) / lengthscale
FLOOR = 1e-30
COST = dict(first=5, load=0.001, stage=0.001, tree=3, own=1, join=1, merge=5, halo=5, rest=1, top=0.001, finish=0.001)
VMEM_LIMIT = 16 * 1024 * 1024
f32 = jnp.float32
bf16 = jnp.bfloat16
VMEM = pl.BlockSpec(memory_space=pltpu.VMEM)
SMEM = pl.BlockSpec(memory_space=pltpu.SMEM)
ANY = pl.BlockSpec(memory_space=pl.ANY)
HBM = pl.BlockSpec(memory_space=pltpu.HBM)


def features(coords, centre):
    shifted = (coords - centre) * KAPPA
    high = shifted.astype(bf16).astype(f32)
    low = (shifted - high).astype(bf16).astype(f32)
    both = high + low
    norm = jnp.sum(both * both, axis=0, keepdims=True)
    first = norm.astype(bf16).astype(f32)
    second = (norm - first).astype(bf16).astype(f32)
    third = norm - first - second
    row = lax.broadcasted_iota(jnp.int32, coords.shape, 0)
    one = jnp.ones_like(coords)
    nil = jnp.zeros_like(coords)

    def six(a, b, c, d, e, f):
        out = jnp.where(row == 0, a, jnp.where(row == 1, b, jnp.where(row == 2, c, nil)))
        return jnp.where(row == 3, d, jnp.where(row == 4, e, jnp.where(row == 5, f, out)))

    left = [-2 * high, -2 * high, -2 * low, -2 * low, six(first, second, third, one, one, one), nil]
    right = [high, low, high, low, six(one, one, one, first, second, third), nil]
    return jnp.concatenate(left, axis=0), jnp.concatenate(right, axis=0).astype(bf16)


def kernel_values(squares):
    squares = jnp.maximum(squares, FLOOR)
    return jnp.exp2(-(squares * lax.rsqrt(squares))).astype(bf16)


def dot(a, b):
    return jnp.dot(a, b, preferred_element_type=f32)


def choose(coords, pivots):
    place = lax.broadcasted_iota(jnp.int32, (coords.shape[1], pivots.shape[1]), 0)
    return dot(coords.astype(bf16), jnp.where(place == pivots, 1.0, 0.0).astype(bf16))


def lanes(*parts):
    return jnp.concatenate(parts, axis=1)


def centre_of(coords):
    return jnp.mean(coords.astype(f32), axis=1, keepdims=True)


def position():
    tile = lax.axis_index("tile")
    return lax.axis_index("cluster"), lax.rem(tile, 2), tile


def load_kernel(*refs):
    count = len(refs) // 2
    for copy in start_copies(list(zip(refs[:count], refs[count:])), refs[-1]):
        copy.wait()


def stage_kernel(points, got1, charges, mate, after, to_send, joined):
    boxes, feat, rows = got1.shape
    joined[:, :rows, :] = charges[...]
    joined[:, rows:, :] = mate[...]
    count = boxes // 2
    start = jnp.where(position()[1] == 0, boxes - count, 0)
    coords = []
    for i in range(count):
        box = start + i
        to_send[2 * i * rows : (2 * i + 1) * rows, :] = charges[box]
        to_send[(2 * i + 1) * rows : 2 * (i + 1) * rows, :] = mate[box]
        coords.append(lanes(points[box], got1[box]).astype(f32))
    to_send[2 * count * rows :, :] = jnp.concatenate(coords, axis=0).astype(bf16)


def with_coords(weights, coords):
    return jnp.concatenate([weights, coords, jnp.zeros_like(coords)], axis=0).astype(bf16)


def tree_kernel(pts0, pts1, pts2, pts3, joined, leaf_pv, merge_pv, *refs):
    outs, held = refs[:4], refs[4]
    half = leaf_pv.shape[0] // 2
    rows = pts0.shape[2]
    _, group, tile = position()
    centre = centre_of(pts0[half])
    coords, weights = [], []
    for i in range(half):
        box = group * half + i
        whole = lanes(pts0[box], pts1[box], pts2[box], pts3[box]).astype(f32)
        chosen = choose(whole, leaf_pv[pl.ds(box, 1), :] ^ (tile * rows))
        left, _ = features(chosen, centre)
        _, right = features(whole[:, : 2 * rows], centre)
        values = kernel_values(dot(left.T.astype(bf16), right))
        coords.append(chosen)
        weights.append(dot(values, joined[box]))
    level = 0
    while len(coords) > 1:
        next_coords, next_weights = [], []
        for i in range(len(coords) // 2):
            cand = lanes(coords[2 * i], coords[2 * i + 1])
            pair = group * (half // 2) + i * 2**level
            chosen = choose(cand, merge_pv[level, pl.ds(pair, 1), :])
            left, _ = features(chosen, centre)
            _, right = features(cand, centre)
            values = kernel_values(dot(left.T.astype(bf16), right))
            charge = jnp.concatenate([weights[2 * i], weights[2 * i + 1]], axis=0).astype(bf16)
            next_coords.append(chosen)
            next_weights.append(dot(values, charge))
        coords, weights = next_coords, next_weights
        level += 1
    held[...] = weights[0].T
    width = held.shape[0] // 4
    for d, out in enumerate(outs):
        out[...] = with_coords(held[pl.ds(pl.multiple_of((tile ^ d) * width, width), width), :], coords[0])


def merged_pair(ours, theirs, our_coords, their_coords, pivots, near=False):
    coords = lanes(our_coords.astype(f32)[:8], their_coords.astype(f32)[:8])
    chosen = choose(coords, pivots)
    if near:
        centre = centre_of(coords)
        left, right = features(coords, centre)[0], features(chosen, centre)[1]
        return dot(lanes(ours, theirs), kernel_values(dot(left.T.astype(bf16), right))), chosen
    across = coords.T
    squares = None
    for f in range(coords.shape[0]):
        diff = across[:, f : f + 1] - chosen[f : f + 1, :]
        squares = diff * diff if squares is None else squares + diff * diff
    values = kernel_values(squares * (KAPPA * KAPPA))
    return dot(lanes(ours, theirs), values), chosen


def join_kernel(level, mine, got1, got2, got3, merge_pv, after, out):
    width = mine.shape[0] - 16
    _, group, _ = position()
    ours = (mine[:width, :].astype(f32) + got2[:width, :].astype(f32)).astype(bf16)
    theirs = (got1[:width, :].astype(f32) + got3[:width, :].astype(f32)).astype(bf16)
    pivots = merge_pv[level, :1, :] ^ (group * mine.shape[1])
    out[...] = with_coords(*merged_pair(ours, theirs, mine[width:, :], got1[width:, :], pivots, True))


def upper_half(bit):
    return lax.rem(lax.div(lax.axis_index("cluster"), 2**bit), 2)


def merge_kernel(level, bit, mine, got, merge_pv, after, out):
    width = mine.shape[0] - 16
    pivots = merge_pv[level, :1, :] ^ (upper_half(bit) * mine.shape[1])
    merged, chosen = merged_pair(mine[:width, :], got[:width, :], mine[width:, :], got[width:, :], pivots)
    ahead = merge_pv[level + 1, :1, :]
    row = lax.broadcasted_iota(jnp.int32, chosen.shape, 0)
    digits = jnp.where(row == 0, ahead & 255, jnp.where(row == 1, ahead >> 8, 0)).astype(f32)
    out[...] = jnp.concatenate([merged, chosen, digits], axis=0).astype(bf16)


def top_kernel(level, bit, mine, got1, got2, got3, merge_pv, out):
    width, rank = mine.shape[0] - 16, mine.shape[1]
    flip = upper_half(bit) * rank
    digits = got2[width:, :].astype(f32)[8:].astype(jnp.int32)
    pairs = []
    for left, right, pivots in (
        (mine, got1, merge_pv[level, :1, :]),
        (got2, got3, digits[0:1] + 256 * digits[1:2]),
    ):
        merged, chosen = merged_pair(
            left[:width, :], right[:width, :], left[width:, :], right[width:, :], pivots ^ flip
        )
        pairs.append((merged.astype(bf16), chosen))
    (ours, our_coords), (theirs, their_coords) = pairs
    pivots = merge_pv[level + 1, :1, :] ^ (upper_half(bit + 1) * rank)
    out[...] = merged_pair(ours, theirs, our_coords, their_coords, pivots)[0].astype(bf16)


def start_copies(pairs, sem):
    copies = [pltpu.make_async_copy(one, other, sem.at[i]) for i, (one, other) in enumerate(pairs)]
    for copy in copies:
        copy.start()
    return copies


def collect(ids, count, base, slots_of, boxes_of, wanted, place, pad, list_v, list_n):
    found = 0
    for v, box in zip(slots_of, boxes_of):
        used = count[box]
        for slot in range(1, ids.shape[1]):
            n = ids[box, slot] - base
            list_v[found] = v
            list_n[found] = place(n)
            found = found + ((slot < used) & wanted(n)).astype(jnp.int32)
    for i in range(3):
        list_v[found + i] = slots_of[0]
        list_n[found + i] = pad
    return found


def for_each(found, add):
    eights = lax.div(found, 8)
    rest = found - 8 * eights
    fours = lax.div(rest + 1, 4)
    twos = lax.div(rest - 4 * fours + 1, 2)

    def run(first, steps, size):
        def step(i, _):
            for k in range(size):
                add(first + size * i + k)
            return 0

        lax.fori_loop(0, steps, step, 0)

    run(0, eights, 8)
    run(8 * eights, fours, 4)
    run(8 * eights + 4 * fours, twos, 2)


def far_row(right):
    row = lax.broadcasted_iota(jnp.int32, right.shape, 0)
    return jnp.where(row == 35, 1e30, 0.0).astype(bf16)


def near_own_kernel(part, all_ids, all_counts, pts0, pts1, pts2, pts3, joined, *refs):
    after, out, left_ref, right_ref, list_v, list_n, ids, count, sem = refs[3 * part :]
    copies = start_copies([(all_ids, ids), (all_counts, count)], sem)
    boxes = joined.shape[0]
    half = boxes // 2
    pair = half // 2
    cluster, group, _ = position()
    centre = centre_of(pts0[half])
    if part == 0:
        for n in range(boxes):
            right_ref[n] = features(lanes(pts0[n], pts1[n]).astype(f32), centre)[1]
        right_ref[boxes] = far_row(right_ref[0])
    mine = [part * pair + v for v in range(pair)]
    order = [group * half + v for v in mine]
    for v, box in zip(mine, order):
        whole = lanes(pts0[box], pts1[box], pts2[box], pts3[box]).astype(f32)
        left_ref[v] = features(whole, centre)[0].T.astype(bf16)

    def one(v, n):
        return dot(kernel_values(dot(left_ref[v], right_ref[n])), joined[jnp.minimum(n, boxes - 1)])

    for v, box in zip(mine, order):
        out[v] = one(v, box)
    for copy in copies:
        copy.wait()
    found = collect(
        ids, count, cluster * boxes, mine, order, lambda n: (n >= 0) & (n < boxes), lambda n: n, boxes, list_v, list_n
    )

    def add(i):
        v = list_v[i]
        out[v] += one(v, list_n[i])

    for_each(found, add)


def near_halo_kernel(part, all_ids, all_counts, pts0, total, left_ref, halo, after, *refs):
    if part == 0:
        send1, send2, send3, acc, right_ref, mark, list_v, list_n, ids, count, sem = refs
    else:
        right_ref, keep, acc, list_v, list_n, ids, count, sem = refs
    copies = start_copies([(all_ids, ids), (all_counts, count)], sem)
    boxes, feat, rows = pts0.shape
    half = boxes // 2
    cluster, group, _ = position()
    if part == 0:
        centre = centre_of(pts0[half])
        coords = halo[2 * half * rows :, :].astype(f32)
        for h in range(half):
            right_ref[h] = features(coords[h * feat : (h + 1) * feat], centre)[1]
        right_ref[half] = far_row(right_ref[0])
    order = [group * half + v for v in range(half)]
    for copy in copies:
        copy.wait()
    found = collect(
        ids,
        count,
        cluster * boxes,
        range(half),
        order,
        lambda n: (n < 0) | (n >= boxes),
        lambda n: jnp.where(group == 0, n + half, n - boxes),
        half,
        list_v,
        list_n,
    )
    mine = slice(0, rows) if part else slice(rows, 4 * rows)

    def add(i):
        v = list_v[i]
        h = list_n[i]
        values = kernel_values(dot(left_ref[v, mine, :], right_ref[h]))
        start = pl.multiple_of(jnp.minimum(h, half - 1) * (2 * rows), 2 * rows)
        acc[v, mine, :] += dot(values, halo[pl.ds(start, 2 * rows), :])

    for_each(found, add)
    if part == 0:
        mark[...] = jnp.zeros_like(mark)
        for d, send in enumerate((send1, send2, send3)):
            send[...] = acc[:, (d + 1) * rows : (d + 2) * rows, :].astype(bf16)
    else:
        keep[...] = acc[:, :rows, :]


def pass_kernel(given, *refs):
    refs[-1][...] = given[...]


def finish_kernel(keep, back1, back2, back3, wide, near, top, held, sem, top_sem):
    half = held.shape[0] // 2
    _, group, _ = position()
    copies = [pltpu.make_async_copy(wide, top.at[0], top_sem)]
    copies[0].start()
    for side, (one, two) in enumerate(((keep, back2), (back1, back3))):
        for i in range(half):
            j = side * half + i
            held[j] = (one[i].astype(f32) + two[i].astype(f32)).astype(bf16)
            copies.append(pltpu.make_async_copy(held.at[j], near.at[(group ^ side) * half + i], sem.at[j]))
            copies[-1].start()
    for copy in copies:
        copy.wait()


def call(body, out_shape, specs, micros, scratch=(), aliases={}, out_spec=VMEM):
    return pl.pallas_call(
        body,
        out_shape=out_shape,
        in_specs=specs,
        out_specs=jax.tree.map(lambda _: out_spec, out_shape),
        scratch_shapes=list(scratch),
        input_output_aliases=aliases,
        compiler_params=pltpu.CompilerParams(vmem_limit_bytes=VMEM_LIMIT),
        cost_estimate=pl.CostEstimate(flops=int(micros * 1.1e9), bytes_accessed=1024, transcendentals=0),
    )


def on_device(points, charges, near_ids, near_count, leaf_pivots, merge_pivots):
    boxes, feat, rows = points.shape
    probes = charges.shape[2]
    rank = leaf_pivots.shape[1]
    half = boxes // 2
    pair = half // 2
    tiles = lax.axis_size("tile")
    clusters = lax.axis_size("cluster")
    local_levels = boxes.bit_length() - 1

    def to_tile(x, d):
        return lax.ppermute(x, "tile", [(i, i ^ d) for i in range(tiles)])

    def to_halo(x):
        route = []
        for i in range(clusters):
            for k in range(tiles):
                target = i + 1 if k % 2 == 0 else i - 1
                if 0 <= target < clusters:
                    route.append((i * tiles + k, target * tiles + k))
        return lax.ppermute(x, ("cluster", "tile"), route)

    def partner(x, stride):
        route = [(i, i ^ stride) for i in range(clusters) if i ^ stride < clusters]
        return lax.ppermute(x, "cluster", route)

    def shape(*dims, dtype=bf16):
        return jax.ShapeDtypeStruct(dims, dtype)

    got = [to_tile(points, d) for d in range(1, 4)]
    mate = to_tile(charges, 1)
    got[2] = call(pass_kernel, shape(*points.shape), [VMEM], COST["first"])(got[2])
    merge_pv = jnp.transpose(merge_pivots, (1, 0, 2))
    arguments = [points, charges, leaf_pivots, merge_pv, near_ids, near_count]
    points, charges, leaf_pv, merge_pv, near_ids, near_count = call(
        load_kernel,
        tuple(jax.ShapeDtypeStruct(x.shape, x.dtype) for x in arguments),
        [HBM] * len(arguments),
        COST["load"],
        [pltpu.SemaphoreType.DMA((len(arguments),))],
    )(*[pltpu.with_memory_space_constraint(x, pltpu.HBM) for x in arguments])
    to_send, joined = call(
        stage_kernel, (shape(half * (2 * rows + feat), probes), shape(boxes, 2 * rows, probes)), [VMEM] * 4 + [ANY], COST["stage"]
    )(points, got[0], charges, mate, got[2])
    halo = to_halo(to_send)
    pts = [points] + got

    width = probes // tiles
    wide_shape = shape(width + 16, rank)
    mine, *sends = call(tree_kernel, (wide_shape,) * 4, [VMEM] * 7, COST["tree"], [pltpu.VMEM((probes, rank), f32)])(
        *pts, joined, leaf_pv, merge_pv
    )
    others = [to_tile(sends[d - 1], d) for d in range(1, 4)]

    lists = [pltpu.SMEM((half * near_ids.shape[1] + 4,), jnp.int32)] * 2
    lists += [pltpu.SMEM(x.shape, jnp.int32) for x in (near_ids, near_count)] + [pltpu.SemaphoreType.DMA((2,))]

    sums = (
        shape(half, 4 * rows, probes, dtype=f32),
        shape(half, 4 * rows, 48),
        shape(boxes + 1, 48, 2 * rows),
    )

    def near_own(part, begun, after):
        specs = [ANY] * 2 + [VMEM] * (5 + len(begun)) + [ANY]
        aliases = {7 + i: i for i in range(len(begun))}
        return call(functools.partial(near_own_kernel, part), sums, specs, COST["own"], lists, aliases)(
            near_ids, near_count, *pts, joined, *begun, after
        )

    begun = near_own(0, [], mine)
    wide = call(functools.partial(join_kernel, local_levels - 1), wide_shape, [VMEM] * 5 + [ANY], COST["join"])(
        mine, *others, merge_pv, begun[2]
    )
    total, left, _ = near_own(1, begun, wide)
    other = partner(wide, 1)
    quarter = shape(half, rows, probes)
    inputs = (near_ids, near_count, points)
    *sends, total, right, mark = call(
        functools.partial(near_halo_kernel, 0),
        (quarter, quarter, quarter, sums[0], shape(half + 1, 48, 2 * rows), shape(16, 128)),
        [ANY] * 2 + [VMEM] * 4 + [ANY],
        COST["halo"],
        lists,
        {3: 3},
    )(*inputs, total, left, halo, left)
    back2, back3, back1 = [to_tile(sends[d - 1], d) for d in (2, 3, 1)]
    back = [back1, back2, back3]
    keep, _ = call(
        functools.partial(near_halo_kernel, 1),
        (shape(half, rows, probes, dtype=f32), sums[0]),
        [ANY] * 2 + [VMEM] * 4 + [ANY, VMEM],
        COST["rest"],
        lists,
        {3: 1},
    )(*inputs, total, left, halo, back[0], right)

    wide = call(functools.partial(merge_kernel, local_levels, 0), wide_shape, [VMEM] * 3 + [ANY], COST["merge"])(
        wide, other, merge_pv, to_tile(mark, 1)
    )
    wide = call(pass_kernel, wide_shape, [VMEM, ANY], COST["load"])(wide, back[0])
    top = call(functools.partial(top_kernel, local_levels + 1, 1), shape(width, rank), [VMEM] * 5, COST["top"])(
        wide, partner(wide, 2), partner(wide, 4), partner(wide, 6), merge_pv
    )
    near, top = call(
        finish_kernel,
        (shape(boxes, rows, probes), shape(1, width, rank)),
        [VMEM] * 5,
        COST["finish"],
        [pltpu.VMEM((boxes, rows, probes), bf16), pltpu.SemaphoreType.DMA((boxes,)), pltpu.SemaphoreType.DMA],
        {},
        HBM,
    )(keep, *back, top)
    return near, jnp.swapaxes(top, 1, 2)


def solution(mesh):
    return jax.shard_map(
        on_device,
        mesh=mesh,
        in_specs=(
            P("cluster", None, "tile"),
            P("cluster", "tile", None),
            P("cluster", None),
            P("cluster"),
            P("cluster", None),
            P("cluster", None, None),
        ),
        out_specs=(P("cluster", "tile", None), P("cluster", None, "tile")),
        check_vma=False,
    )
```

```python
import functools
import math

import jax
import jax.numpy as jnp
from jax import lax
from jax.experimental import pallas as pl
from jax.experimental.pallas import tpu as pltpu
from jax.sharding import PartitionSpec as P

SPAN = 4
lengthscale = 0.7
KAPPA = math.log2(math.e) / lengthscale
FLOOR = 1e-30
COST = dict(first=5, load=0.001, stage=0.001, tree=3, own=1, join=1, merge=5, halo=5, rest=1, top=0.001, finish=0.001)
VMEM_LIMIT = 16 * 1024 * 1024
f32 = jnp.float32
bf16 = jnp.bfloat16
VMEM = pl.BlockSpec(memory_space=pltpu.VMEM)
SMEM = pl.BlockSpec(memory_space=pltpu.SMEM)
ANY = pl.BlockSpec(memory_space=pl.ANY)
HBM = pl.BlockSpec(memory_space=pltpu.HBM)


def features(coords, centre):
    shifted = (coords - centre) * KAPPA
    high = shifted.astype(bf16).astype(f32)
    low = (shifted - high).astype(bf16).astype(f32)
    both = high + low
    norm = jnp.sum(both * both, axis=0, keepdims=True)
    first = norm.astype(bf16).astype(f32)
    second = (norm - first).astype(bf16).astype(f32)
    third = norm - first - second
    row = lax.broadcasted_iota(jnp.int32, coords.shape, 0)
    one = jnp.ones_like(coords)
    nil = jnp.zeros_like(coords)

    def six(a, b, c, d, e, f):
        out = jnp.where(row == 0, a, jnp.where(row == 1, b, jnp.where(row == 2, c, nil)))
        return jnp.where(row == 3, d, jnp.where(row == 4, e, jnp.where(row == 5, f, out)))

    left = [-2 * high, -2 * high, -2 * low, -2 * low, six(first, second, third, one, one, one), nil]
    right = [high, low, high, low, six(one, one, one, first, second, third), nil]
    return jnp.concatenate(left, axis=0), jnp.concatenate(right, axis=0).astype(bf16)


def kernel_values(squares):
    squares = jnp.maximum(squares, FLOOR)
    return jnp.exp2(-(squares * lax.rsqrt(squares))).astype(bf16)


def dot(a, b):
    return jnp.dot(a, b, preferred_element_type=f32)


def choose(coords, pivots):
    place = lax.broadcasted_iota(jnp.int32, (coords.shape[1], pivots.shape[1]), 0)
    return dot(coords.astype(bf16), jnp.where(place == pivots, 1.0, 0.0).astype(bf16))


def lanes(*parts):
    return jnp.concatenate(parts, axis=1)


def centre_of(coords):
    return jnp.mean(coords.astype(f32), axis=1, keepdims=True)


def position():
    tile = lax.axis_index("tile")
    return lax.axis_index("cluster"), lax.rem(tile, 2), tile


def load_kernel(*refs):
    count = len(refs) // 2
    for copy in start_copies(list(zip(refs[:count], refs[count:])), refs[-1]):
        copy.wait()


def stage_kernel(points, got1, charges, mate, after, to_send, joined):
    boxes, feat, rows = got1.shape
    joined[:, :rows, :] = charges[...]
    joined[:, rows:, :] = mate[...]
    count = boxes // 2
    start = jnp.where(position()[1] == 0, boxes - count, 0)
    coords = []
    for i in range(count):
        box = start + i
        to_send[2 * i * rows : (2 * i + 1) * rows, :] = charges[box]
        to_send[(2 * i + 1) * rows : 2 * (i + 1) * rows, :] = mate[box]
        coords.append(lanes(points[box], got1[box]).astype(f32))
    to_send[2 * count * rows :, :] = jnp.concatenate(coords, axis=0).astype(bf16)


def with_coords(weights, coords):
    return jnp.concatenate([weights, coords, jnp.zeros_like(coords)], axis=0).astype(bf16)


def tree_kernel(pts0, pts1, pts2, pts3, joined, leaf_pv, merge_pv, *refs):
    outs, held = refs[:4], refs[4]
    half = leaf_pv.shape[0] // 2
    rows = pts0.shape[2]
    _, group, tile = position()
    centre = centre_of(pts0[half])
    coords, weights = [], []
    for i in range(half):
        box = group * half + i
        whole = lanes(pts0[box], pts1[box], pts2[box], pts3[box]).astype(f32)
        chosen = choose(whole, leaf_pv[pl.ds(box, 1), :] ^ (tile * rows))
        left, _ = features(chosen, centre)
        _, right = features(whole[:, : 2 * rows], centre)
        values = kernel_values(dot(left.T.astype(bf16), right))
        coords.append(chosen)
        weights.append(dot(values, joined[box]))
    level = 0
    while len(coords) > 1:
        next_coords, next_weights = [], []
        for i in range(len(coords) // 2):
            cand = lanes(coords[2 * i], coords[2 * i + 1])
            pair = group * (half // 2) + i * 2**level
            chosen = choose(cand, merge_pv[level, pl.ds(pair, 1), :])
            left, _ = features(chosen, centre)
            _, right = features(cand, centre)
            values = kernel_values(dot(left.T.astype(bf16), right))
            charge = jnp.concatenate([weights[2 * i], weights[2 * i + 1]], axis=0).astype(bf16)
            next_coords.append(chosen)
            next_weights.append(dot(values, charge))
        coords, weights = next_coords, next_weights
        level += 1
    held[...] = weights[0].T
    width = held.shape[0] // 4
    for d, out in enumerate(outs):
        out[...] = with_coords(held[pl.ds(pl.multiple_of((tile ^ d) * width, width), width), :], coords[0])


def merged_pair(ours, theirs, our_coords, their_coords, pivots, near=False):
    coords = lanes(our_coords.astype(f32)[:8], their_coords.astype(f32)[:8])
    chosen = choose(coords, pivots)
    if near:
        centre = centre_of(coords)
        left, right = features(coords, centre)[0], features(chosen, centre)[1]
        return dot(lanes(ours, theirs), kernel_values(dot(left.T.astype(bf16), right))), chosen
    across = coords.T
    squares = None
    for f in range(coords.shape[0]):
        diff = across[:, f : f + 1] - chosen[f : f + 1, :]
        squares = diff * diff if squares is None else squares + diff * diff
    values = kernel_values(squares * (KAPPA * KAPPA))
    return dot(lanes(ours, theirs), values), chosen


def join_kernel(level, mine, got1, got2, got3, merge_pv, after, out):
    width = mine.shape[0] - 16
    _, group, _ = position()
    ours = (mine[:width, :].astype(f32) + got2[:width, :].astype(f32)).astype(bf16)
    theirs = (got1[:width, :].astype(f32) + got3[:width, :].astype(f32)).astype(bf16)
    pivots = merge_pv[level, :1, :] ^ (group * mine.shape[1])
    out[...] = with_coords(*merged_pair(ours, theirs, mine[width:, :], got1[width:, :], pivots, True))


def upper_half(bit):
    return lax.rem(lax.div(lax.axis_index("cluster"), 2**bit), 2)


def merge_kernel(level, bit, mine, got, merge_pv, after, out):
    width = mine.shape[0] - 16
    pivots = merge_pv[level, :1, :] ^ (upper_half(bit) * mine.shape[1])
    merged, chosen = merged_pair(mine[:width, :], got[:width, :], mine[width:, :], got[width:, :], pivots)
    ahead = merge_pv[level + 1, :1, :]
    row = lax.broadcasted_iota(jnp.int32, chosen.shape, 0)
    digits = jnp.where(row == 0, ahead & 255, jnp.where(row == 1, ahead >> 8, 0)).astype(f32)
    out[...] = jnp.concatenate([merged, chosen, digits], axis=0).astype(bf16)


def near_pair_kernel(level, bit, mine, got, merge_pv, out):
    width = mine.shape[0] - 16
    pivots = merge_pv[level, :1, :] ^ (upper_half(bit) * mine.shape[1])
    out[...] = with_coords(
        *merged_pair(mine[:width, :], got[:width, :], mine[width:, :], got[width:, :], pivots)
    )


def top_kernel(level, bit, pair, got2, got3, merge_pv, out):
    width, rank = pair.shape[0] - 16, pair.shape[1]
    digits = got2[width:, :].astype(f32)[8:].astype(jnp.int32)
    pivots = (digits[0:1] + 256 * digits[1:2]) ^ (upper_half(bit) * rank)
    merged, chosen = merged_pair(got2[:width, :], got3[:width, :], got2[width:, :], got3[width:, :], pivots)
    pivots = merge_pv[level + 1, :1, :] ^ (upper_half(bit + 1) * rank)
    out[...] = merged_pair(pair[:width, :], merged.astype(bf16), pair[width:, :], chosen, pivots)[0].astype(bf16)


def start_copies(pairs, sem):
    copies = [pltpu.make_async_copy(one, other, sem.at[i]) for i, (one, other) in enumerate(pairs)]
    for copy in copies:
        copy.start()
    return copies


def collect(ids, count, base, slots_of, boxes_of, wanted, place, pad, list_v, list_n):
    found = 0
    for v, box in zip(slots_of, boxes_of):
        used = count[box]
        for slot in range(1, ids.shape[1]):
            n = ids[box, slot] - base
            list_v[found] = v
            list_n[found] = place(n)
            found = found + ((slot < used) & wanted(n)).astype(jnp.int32)
    for i in range(3):
        list_v[found + i] = slots_of[0]
        list_n[found + i] = pad
    return found


def for_each(found, add):
    eights = lax.div(found, 8)
    rest = found - 8 * eights
    fours = lax.div(rest + 1, 4)
    twos = lax.div(rest - 4 * fours + 1, 2)

    def run(first, steps, size):
        def step(i, _):
            for k in range(size):
                add(first + size * i + k)
            return 0

        lax.fori_loop(0, steps, step, 0)

    run(0, eights, 8)
    run(8 * eights, fours, 4)
    run(8 * eights + 4 * fours, twos, 2)


def far_row(right):
    row = lax.broadcasted_iota(jnp.int32, right.shape, 0)
    return jnp.where(row == 35, 1e30, 0.0).astype(bf16)


def near_own_kernel(part, all_ids, all_counts, pts0, pts1, pts2, pts3, joined, *refs):
    after, out, left_ref, right_ref, list_v, list_n, ids, count, sem = refs[3 * part :]
    copies = start_copies([(all_ids, ids), (all_counts, count)], sem)
    boxes = joined.shape[0]
    half = boxes // 2
    pair = half // 2
    cluster, group, _ = position()
    centre = centre_of(pts0[half])
    if part == 0:
        for n in range(boxes):
            right_ref[n] = features(lanes(pts0[n], pts1[n]).astype(f32), centre)[1]
        right_ref[boxes] = far_row(right_ref[0])
    mine = [part * pair + v for v in range(pair)]
    order = [group * half + v for v in mine]
    for v, box in zip(mine, order):
        whole = lanes(pts0[box], pts1[box], pts2[box], pts3[box]).astype(f32)
        left_ref[v] = features(whole, centre)[0].T.astype(bf16)

    def one(v, n):
        return dot(kernel_values(dot(left_ref[v], right_ref[n])), joined[jnp.minimum(n, boxes - 1)])

    for v, box in zip(mine, order):
        out[v] = one(v, box)
    for copy in copies:
        copy.wait()
    found = collect(
        ids, count, cluster * boxes, mine, order, lambda n: (n >= 0) & (n < boxes), lambda n: n, boxes, list_v, list_n
    )

    def add(i):
        v = list_v[i]
        out[v] += one(v, list_n[i])

    for_each(found, add)


def near_halo_kernel(part, all_ids, all_counts, pts0, total, left_ref, halo, after, *refs):
    if part == 0:
        send1, send2, send3, acc, right_ref, mark, list_v, list_n, ids, count, sem = refs
    else:
        right_ref, keep, acc, list_v, list_n, ids, count, sem = refs
    copies = start_copies([(all_ids, ids), (all_counts, count)], sem)
    boxes, feat, rows = pts0.shape
    half = boxes // 2
    cluster, group, _ = position()
    if part == 0:
        centre = centre_of(pts0[half])
        coords = halo[2 * half * rows :, :].astype(f32)
        for h in range(half):
            right_ref[h] = features(coords[h * feat : (h + 1) * feat], centre)[1]
        right_ref[half] = far_row(right_ref[0])
    order = [group * half + v for v in range(half)]
    for copy in copies:
        copy.wait()
    found = collect(
        ids,
        count,
        cluster * boxes,
        range(half),
        order,
        lambda n: (n < 0) | (n >= boxes),
        lambda n: jnp.where(group == 0, n + half, n - boxes),
        half,
        list_v,
        list_n,
    )
    mine = slice(0, rows) if part else slice(rows, 4 * rows)

    def add(i):
        v = list_v[i]
        h = list_n[i]
        values = kernel_values(dot(left_ref[v, mine, :], right_ref[h]))
        start = pl.multiple_of(jnp.minimum(h, half - 1) * (2 * rows), 2 * rows)
        acc[v, mine, :] += dot(values, halo[pl.ds(start, 2 * rows), :])

    for_each(found, add)
    if part == 0:
        mark[...] = jnp.zeros_like(mark)
        for d, send in enumerate((send1, send2, send3)):
            send[...] = acc[:, (d + 1) * rows : (d + 2) * rows, :].astype(bf16)
    else:
        keep[...] = acc[:, :rows, :]


def pass_kernel(given, *refs):
    refs[-1][...] = given[...]


def finish_kernel(keep, back1, back2, back3, wide, near, top, held, sem, top_sem):
    half = held.shape[0] // 2
    _, group, _ = position()
    copies = [pltpu.make_async_copy(wide, top.at[0], top_sem)]
    copies[0].start()
    for side, (one, two) in enumerate(((keep, back2), (back1, back3))):
        for i in range(half):
            j = side * half + i
            held[j] = (one[i].astype(f32) + two[i].astype(f32)).astype(bf16)
            copies.append(pltpu.make_async_copy(held.at[j], near.at[(group ^ side) * half + i], sem.at[j]))
            copies[-1].start()
    for copy in copies:
        copy.wait()


def call(body, out_shape, specs, micros, scratch=(), aliases={}, out_spec=VMEM):
    return pl.pallas_call(
        body,
        out_shape=out_shape,
        in_specs=specs,
        out_specs=jax.tree.map(lambda _: out_spec, out_shape),
        scratch_shapes=list(scratch),
        input_output_aliases=aliases,
        compiler_params=pltpu.CompilerParams(vmem_limit_bytes=VMEM_LIMIT),
        cost_estimate=pl.CostEstimate(flops=int(micros * 1.1e9), bytes_accessed=1024, transcendentals=0),
    )


def on_device(points, charges, near_ids, near_count, leaf_pivots, merge_pivots):
    boxes, feat, rows = points.shape
    probes = charges.shape[2]
    rank = leaf_pivots.shape[1]
    half = boxes // 2
    pair = half // 2
    tiles = lax.axis_size("tile")
    clusters = lax.axis_size("cluster")
    local_levels = boxes.bit_length() - 1

    def to_tile(x, d):
        return lax.ppermute(x, "tile", [(i, i ^ d) for i in range(tiles)])

    def to_halo(x):
        route = []
        for i in range(clusters):
            for k in range(tiles):
                target = i + 1 if k % 2 == 0 else i - 1
                if 0 <= target < clusters:
                    route.append((i * tiles + k, target * tiles + k))
        return lax.ppermute(x, ("cluster", "tile"), route)

    def partner(x, stride):
        route = [(i, i ^ stride) for i in range(clusters) if i ^ stride < clusters]
        return lax.ppermute(x, "cluster", route)

    def shape(*dims, dtype=bf16):
        return jax.ShapeDtypeStruct(dims, dtype)

    got = [to_tile(points, d) for d in range(1, 4)]
    mate = to_tile(charges, 1)
    got[2] = call(pass_kernel, shape(*points.shape), [VMEM], COST["first"])(got[2])
    merge_pv = jnp.transpose(merge_pivots, (1, 0, 2))
    arguments = [points, charges, leaf_pivots, merge_pv, near_ids, near_count]
    points, charges, leaf_pv, merge_pv, near_ids, near_count = call(
        load_kernel,
        tuple(jax.ShapeDtypeStruct(x.shape, x.dtype) for x in arguments),
        [HBM] * len(arguments),
        COST["load"],
        [pltpu.SemaphoreType.DMA((len(arguments),))],
    )(*[pltpu.with_memory_space_constraint(x, pltpu.HBM) for x in arguments])
    to_send, joined = call(
        stage_kernel, (shape(half * (2 * rows + feat), probes), shape(boxes, 2 * rows, probes)), [VMEM] * 4 + [ANY], COST["stage"]
    )(points, got[0], charges, mate, got[2])
    halo = to_halo(to_send)
    pts = [points] + got

    width = probes // tiles
    wide_shape = shape(width + 16, rank)
    mine, *sends = call(tree_kernel, (wide_shape,) * 4, [VMEM] * 7, COST["tree"], [pltpu.VMEM((probes, rank), f32)])(
        *pts, joined, leaf_pv, merge_pv
    )
    others = [to_tile(sends[d - 1], d) for d in range(1, 4)]

    lists = [pltpu.SMEM((half * near_ids.shape[1] + 4,), jnp.int32)] * 2
    lists += [pltpu.SMEM(x.shape, jnp.int32) for x in (near_ids, near_count)] + [pltpu.SemaphoreType.DMA((2,))]

    sums = (
        shape(half, 4 * rows, probes, dtype=f32),
        shape(half, 4 * rows, 48),
        shape(boxes + 1, 48, 2 * rows),
    )

    def near_own(part, begun, after):
        specs = [ANY] * 2 + [VMEM] * (5 + len(begun)) + [ANY]
        aliases = {7 + i: i for i in range(len(begun))}
        return call(functools.partial(near_own_kernel, part), sums, specs, COST["own"], lists, aliases)(
            near_ids, near_count, *pts, joined, *begun, after
        )

    begun = near_own(0, [], mine)
    wide = call(functools.partial(join_kernel, local_levels - 1), wide_shape, [VMEM] * 5 + [ANY], COST["join"])(
        mine, *others, merge_pv, begun[2]
    )
    total, left, _ = near_own(1, begun, wide)
    other = partner(wide, 1)
    quarter = shape(half, rows, probes)
    inputs = (near_ids, near_count, points)
    *sends, total, right, mark = call(
        functools.partial(near_halo_kernel, 0),
        (quarter, quarter, quarter, sums[0], shape(half + 1, 48, 2 * rows), shape(16, 128)),
        [ANY] * 2 + [VMEM] * 4 + [ANY],
        COST["halo"],
        lists,
        {3: 3},
    )(*inputs, total, left, halo, left)
    back2, back3, back1 = [to_tile(sends[d - 1], d) for d in (2, 3, 1)]
    back = [back1, back2, back3]
    keep, _ = call(
        functools.partial(near_halo_kernel, 1),
        (shape(half, rows, probes, dtype=f32), sums[0]),
        [ANY] * 2 + [VMEM] * 4 + [ANY, VMEM],
        COST["rest"],
        lists,
        {3: 1},
    )(*inputs, total, left, halo, back[0], right)

    wide = call(functools.partial(merge_kernel, local_levels, 0), wide_shape, [VMEM] * 3 + [ANY], COST["merge"])(
        wide, other, merge_pv, to_tile(mark, 1)
    )
    wide = call(pass_kernel, wide_shape, [VMEM, ANY], COST["load"])(wide, back[0])
    near_pair = call(
        functools.partial(near_pair_kernel, local_levels + 1, 1), wide_shape, [VMEM] * 3, COST["top"]
    )(wide, partner(wide, 2), merge_pv)
    top = call(functools.partial(top_kernel, local_levels + 1, 1), shape(width, rank), [VMEM] * 4, COST["top"])(
        near_pair, partner(wide, 4), partner(wide, 6), merge_pv
    )
    near, top = call(
        finish_kernel,
        (shape(boxes, rows, probes), shape(1, width, rank)),
        [VMEM] * 5,
        COST["finish"],
        [pltpu.VMEM((boxes, rows, probes), bf16), pltpu.SemaphoreType.DMA((boxes,)), pltpu.SemaphoreType.DMA],
        {},
        HBM,
    )(keep, *back, top)
    return near, jnp.swapaxes(top, 1, 2)


def solution(mesh):
    return jax.shard_map(
        on_device,
        mesh=mesh,
        in_specs=(
            P("cluster", None, "tile"),
            P("cluster", "tile", None),
            P("cluster", None),
            P("cluster"),
            P("cluster", None),
            P("cluster", None, None),
        ),
        out_specs=(P("cluster", "tile", None), P("cluster", None, "tile")),
        check_vma=False,
    )
```
